32 devices in a mesh: vin: 8 (over z, core), vout: 2 (over x), cell: 2 (over y).
Axes of the slice: x: 2, y: 2, z: 4, core: 2. Of those that a mesh axis runs over, the one named last changes fastest.
Arguments:
- distribution: bfloat16 [8, 13824, 4, 128], P('vout', 'vin', 'cell'), may hold values from -6 to 6
- collision: bfloat16 [13824, 13824], P('vout', 'vin'), may hold values from -1 to 3
- speeds: float32 [3, 13824], P(None, 'vout'), may hold values from 0.05 to 0.3
- directions: int32 [3, 13824], P(None, 'vout'), may hold values from 0 to 1
- cell_flags: int32 [8, 4, 128], P('vin', 'cell'), may hold values 0 or 1
Outputs:
- updated: bfloat16 [8, 13824, 4, 128], P('vin', 'vout', 'cell')
The draws below stay inside these ranges and needn't reach their ends.
Inputs may be any that keep to these rules, and one draw needn't show every extreme that they name: `directions`: 1 means the component is positive, 0 negative. `cell_flags`: 1 marks a solid cell, where nothing is transported.
All inputs are finite; a program needn't handle non-finite values. No bound on the sum of `cell_flags` on one device may be relied on, other than what follows from the above.
Results may differ from the reference program's by a relative error of at most 0.023.
Values may be sent and summed in bfloat16 or wider, within the bound.
A program may use at most 128 MiB of HBM per device.

```python
import jax
import jax.numpy as jnp
from jax import lax

NV = 13824
NX = 128
NZ = 8
NY = 4
N_VIN = 8


def draw_collision(key, part):
    matrix_order = NV
    noise = jnp.clip(jax.random.normal(key, (matrix_order, matrix_order), jnp.float32), -4.0, 4.0)
    diag_value = 1.0
    row_index = lax.broadcasted_iota(jnp.int32, (matrix_order, matrix_order), 0)
    col_index = lax.broadcasted_iota(jnp.int32, (matrix_order, matrix_order), 1)
    identity = jnp.where(row_index == col_index, diag_value, 0.0)
    return (noise * matrix_order ** (-0.5) + identity).astype(jnp.bfloat16)


def touch_ends(values, rng, low, top_value):
    extent = values.shape
    index_at = [jax.random.randint(jax.random.fold_in(rng, axis), (), 0, extent[axis]) for axis in range(len(extent))]
    values = values.at[tuple(index_at)].set(low)
    longest = extent.index(max(extent))
    index_at[longest] = (index_at[longest] + 1) % extent[longest]
    return values.at[tuple(index_at)].set(top_value)


def block_scale(own_key, shape, cuts, low, largest):
    level, own = 1.0, jax.random.fold_in(own_key, 6)
    for position, parts in cuts:
        heights = jnp.exp(jax.random.uniform(jax.random.fold_in(own, position), (parts,), jnp.float32, low / len(cuts), largest / len(cuts)))
        level = level * jnp.repeat(heights, shape[position] // parts).reshape([-1 if axis == position else 1 for axis in range(len(shape))])
    return level


def normal_values(rng, shape, deviation, most, pieces=(), dtype=jnp.bfloat16):
    result = jax.random.normal(rng, shape, jnp.float32) * deviation
    if len(pieces) > 0:
        result = block_scale(rng, shape, pieces, -0.22, 0.18) * result
    return jnp.clip(result, min=-most, max=most).astype(dtype)


def setup_inputs(seed: int = 0) -> dict:
    arg_keys = jax.random.split(jax.random.key(seed), 6)
    distribution = normal_values(arg_keys[0], (NZ, NV, NY, NX), 1.0, 6.0, ((0, 2), (1, 8), (2, 2)))
    collision = draw_collision(jax.random.fold_in(arg_keys[5], 71), 0)
    speeds = jnp.clip(0.05 + 0.25 * jax.random.uniform(arg_keys[2], (3, NV), jnp.float32) ** block_scale(arg_keys[2], (3, NV), ((1, 2),), -0.2, 0.2), 0.05, 0.3)
    directions = touch_ends(jax.random.randint(arg_keys[3], (3, NV), 0, 2), jax.random.fold_in(arg_keys[3], 1), 0, 1).astype(jnp.int32)
    cell_flags = touch_ends((jax.random.randint(arg_keys[4], (NZ, NY, NX), 0, 4) < 1).astype(jnp.int32), jax.random.fold_in(arg_keys[4], 1), 0, 1)
    return dict(distribution=distribution, collision=collision, speeds=speeds, directions=directions, cell_flags=cell_flags)


def transport(padded, speeds, directions, cell_flags):
    field_pad = padded.astype(jnp.float32)
    extended = jnp.pad(field_pad, ((0, 0), (0, 0), (0, 0), (1, 1)))
    center = extended[1:-1, :, 1:-1, 1:-1]
    neighbours = (
        (extended[1:-1, :, 1:-1, :-2], extended[1:-1, :, 1:-1, 2:]),
        (extended[1:-1, :, :-2, 1:-1], extended[1:-1, :, 2:, 1:-1]),
        (extended[:-2, :, 1:-1, 1:-1], extended[2:, :, 1:-1, 1:-1]),
    )
    flux_sum = jnp.zeros_like(center)
    for component in range(3):
        low_side, high_side = neighbours[component]
        positive = (directions[component] == 1)[None, :, None, None]
        upstream = jnp.where(positive, low_side, high_side)
        flux_sum = flux_sum + speeds[component][None, :, None, None] * (center - upstream)
    fluid_mask = (1 - cell_flags).astype(jnp.float32)[:, None, :, :]
    return (center - fluid_mask * flux_sum).astype(jnp.bfloat16)


def reference(distribution, collision, speeds, directions, cell_flags):
    block_size = NV // N_VIN
    dist_wide = distribution.astype(jnp.float32)

    def add_block(index, total):
        offset = jnp.asarray(index, jnp.int32) * block_size
        matrix_cols = lax.dynamic_slice_in_dim(collision, offset, block_size, 1).astype(jnp.float32)
        dist_block = lax.dynamic_slice_in_dim(dist_wide, offset, block_size, 1)
        partial_sum = jnp.einsum("vu,zuyx->zvyx", matrix_cols, dist_block)
        rounded = lax.optimization_barrier(partial_sum.astype(jnp.bfloat16))
        return total + rounded.astype(jnp.float32)

    total = lax.fori_loop(0, N_VIN, add_block, jnp.zeros((NZ, NV, NY, NX), jnp.float32))
    relaxed = total.astype(jnp.bfloat16)
    padded = jnp.pad(relaxed, ((1, 1), (0, 0), (1, 1), (0, 0)))
    return transport(padded, speeds, directions, cell_flags)
```

```python
import functools

import jax
import jax.numpy as jnp
from jax import lax
from jax.experimental import pallas as pl
from jax.experimental.pallas import tpu as pltpu
from jax.sharding import PartitionSpec as P

MESH = pl.DeviceIdType.MESH
CORES = 2
LANES = 128
BLOCK = 16


def rows_of(half):
    for rows in (576, 432, 288, 144, 96, 48, 16):
        if half % rows == 0:
            return rows
    return half


def kernel(
    size, dist, matrix, coef, fluid, out, lent,
    held, tile, sums, slots, weights, fluids,
    l_sem, cs_sem, cr_sem, xs_sem, xr_sem, hs_sem, hr_sem, gs_sem, gr_sem, ms_sem, mr_sem,
    fs_sem, fr_sem, t_sem, zs_sem, zr_sem, ol_sem, os_sem, or_sem,
):
    n, groups, planes, depth, half, rows, pieces = size
    total = n * CORES
    chunks = half // rows
    part = rows // pieces
    wide = 2 * LANES
    vin, x, y = lax.axis_index("vin"), lax.axis_index("vout"), lax.axis_index("cell")
    k, c = vin // CORES, lax.rem(vin, CORES)
    partner = {"vin": k * CORES + 1 - c}
    mirror = 2 * x >= groups
    staged = groups == 2 and n == 4 and planes == 4

    def remote(src, dst, send, recv, where):
        return pltpu.make_async_remote_copy(
            src_ref=src, dst_ref=dst, send_sem=send, recv_sem=recv, device_id=where, device_id_type=MESH
        )

    def other_group(j):
        return lax.rem(x + j, groups)

    everyone = [{"vin": lax.rem(vin + j, total)} for j in range(1, total)]
    for j in range(groups):
        if j:
            everyone.append({"vout": other_group(j)})
        everyone.append({"vout": other_group(j), "cell": 1 - y})
    barrier = pltpu.get_barrier_semaphore()
    for where in everyone:
        pl.semaphore_signal(barrier, inc=1, device_id=where, device_id_type=MESH)
    pl.semaphore_wait(barrier, len(everyone))

    def order(t):
        at = jnp.where(mirror, n - 1 - k, k)
        usual = jnp.where(t < 2, t, n + 1 - t)
        first = jnp.where(t == 0, 1, jnp.where(t == 1, n - 1, jnp.where(t == 2, 0, n + 1 - t)))
        g = jnp.where(at == 0, first, usual)
        return jnp.where(mirror, n - 1 - g, g)

    def item(s):
        j = s - chunks
        early, late = s < chunks, s >= (n - 1) * chunks
        t = jnp.where(early, 0, jnp.where(late, n - 1, 1 + lax.rem(j, n - 2)))
        i = jnp.where(early, s, jnp.where(late, s - (n - 1) * chunks, j // (n - 2)))
        return order(t), i

    mine = pl.ds(pl.multiple_of(c * depth, 16), depth)
    theirs = pl.ds(pl.multiple_of((1 - c) * depth, 16), depth)
    inner = pl.ds(pl.multiple_of((1 - y) * LANES, LANES), LANES)

    def halo_lanes(p):
        return pl.ds(pl.multiple_of(lax.rem(p, 2) * LANES, LANES), LANES)

    def local_plane(q):
        return pltpu.make_async_copy(dist.at[q], held.at[x * planes + q, mine], l_sem.at[q])

    def core_own(q):
        p = x * planes + q
        return remote(dist.at[q], held.at[p, mine], cs_sem.at[p], cr_sem.at[p], partner)

    def core_pass(p):
        return remote(held.at[p, mine], held.at[p, mine], cs_sem.at[p], cr_sem.at[p], partner)

    def core_got(p):
        return remote(held.at[p, theirs], held.at[p, theirs], cs_sem.at[p], cr_sem.at[p], partner)

    def main_send(to, q):
        p = x * planes + q
        return remote(dist.at[q], held.at[p, mine], xs_sem.at[to, q], xr_sem.at[p], {"vout": to})

    def main_got(p):
        return remote(held.at[p, mine], held.at[p, mine], xs_sem.at[0, 0], xr_sem.at[p], {"vout": other_group(1)})

    def halo_send(to, q):
        p = x * planes + q
        return remote(
            dist.at[q, :, inner], held.at[total + p // 2, mine, halo_lanes(p)], hs_sem.at[to, q], hr_sem.at[p],
            {"vout": to, "cell": 1 - y},
        )

    def halo_got(p):
        ref = held.at[total + p // 2, mine, halo_lanes(p)]
        return remote(ref, ref, hs_sem.at[0, 0], hr_sem.at[p], {"cell": 1 - y})

    def halo_pass(p):
        ref = held.at[total + p // 2, mine, halo_lanes(p)]
        return remote(ref, ref, gs_sem.at[p], gr_sem.at[p], partner)

    def halo_end(p):
        ref = held.at[total + p // 2, theirs, halo_lanes(p)]
        return remote(ref, ref, gs_sem.at[p], gr_sem.at[p], partner)

    def own_half(i):
        return pl.ds(pl.multiple_of(c * half + i * rows, 16), rows)

    def matrix_send(i):
        start = pl.multiple_of((1 - c) * half + i * rows, 16)
        return remote(
            matrix.at[pl.ds(start, rows)], lent.at[pl.ds(i * rows, rows)], ms_sem.at[i], mr_sem.at[i], partner
        )

    def flag_send(j):
        to = lax.rem(vin + j, total)
        return remote(fluid, fluids.at[vin], fs_sem.at[to], fr_sem.at[vin], {"vin": to})

    def flag_got(j):
        at = lax.rem(vin + j, total)
        return remote(fluid, fluids.at[at], fs_sem.at[at], fr_sem.at[at], {"vin": at})

    def load(s, which):
        i = item(s)[1]
        slot = lax.rem(s, 2)
        if which == 0:
            src, at = matrix.at[own_half(i)], c
        else:
            src, at = lent.at[pl.ds(pl.multiple_of(i * rows, 16), rows)], 1 - c
        return pltpu.make_async_copy(src, tile.at[slot, at], t_sem.at[slot, which])

    def coef_load():
        return pltpu.make_async_copy(
            coef.at[pl.ds(pl.multiple_of(c * half, 16), half)], weights, l_sem.at[planes]
        )

    first_pair = lax.rem(order(0), planes // 2)

    def halo_order(j):
        if not staged:
            return j
        pair = first_pair if j < 2 else 1 - first_pair
        return pair * 2 + j % 2

    def away(to, j):
        return jnp.where(x > to, j, planes - 1 - j)

    def from_group(src, j):
        return src * planes + jnp.where(src > x, j, planes - 1 - j)

    for q in range(planes):
        core_own(q).start()
        local_plane(q).start()
    for j in range(min(2, planes)):
        halo_send(x, halo_order(j)).start()
    for m in range(1, groups):
        to = other_group(m)
        main_send(to, away(to, 0)).start()
    matrix_send(0).start()
    load(0, 0).start()
    coef_load().start()
    for j in range(1, total):
        flag_send(j).start()
    for i in range(1, chunks):
        matrix_send(i).start()
    for j in range(2, planes):
        halo_send(x, halo_order(j)).start()
    for m in range(1, groups):
        to = other_group(m)
        for j in range(1, planes):
            main_send(to, away(to, j)).start()
        for j in list(range(2, planes)) + list(range(min(2, planes))):
            halo_send(to, away(to, j)).start()
    fluids[vin] = fluid[...]
    mr0 = matrix_send(0)
    mr0.wait_recv()
    load(0, 1).start()
    for j in range(1, total):
        flag_got(j).wait_recv()

    own = [x * planes + halo_order(j) for j in range(planes)]

    def pass_halo(ps):
        for p in ps:
            halo_got(p).wait_recv()
            halo_pass(p).start()

    def end_halo(ps):
        for p in ps:
            halo_end(p).wait_recv()

    def pass_main(ps):
        for p in ps:
            main_got(p).wait_recv()
            core_pass(p).start()

    def end_main(ps):
        for p in ps:
            core_got(p).wait_recv()

    near = [from_group(other_group(m), 0) for m in range(1, groups)]
    far = [from_group(other_group(m), j) for m in range(1, groups) for j in range(1, planes)]
    far_halo = [from_group(other_group(m), j) for m in range(1, groups) for j in range(2, planes)]
    near_halo = [from_group(other_group(m), j) for m in range(1, groups) for j in range(min(2, planes))]

    for q in range(planes):
        local_plane(q).wait()
    coef_load().wait()
    end_main([x * planes + q for q in range(planes)])
    pass_halo(own[:2])
    pass_main(near)
    end_halo(own[:2])
    end_main(near)

    def stage_two():
        pass_halo(own[2:])
        pass_main(far)
        pass_halo(far_halo)
        end_halo(own[2:])
        end_main(far)
        end_halo(far_halo)

    def stage_three():
        pass_halo(near_halo)
        end_halo(near_halo)

    if not staged:
        stage_two()
        stage_three()

    lane = lax.broadcasted_iota(jnp.int32, (BLOCK, LANES), 1)

    def message(g, m):
        up = g > k
        chip = jnp.clip(jnp.where(up, k + 1, k - 1), 0, n - 1)
        slot = jnp.where(up | (chip != g), g, n)
        at = pl.ds(pl.multiple_of(m * part, 16), part)
        return remote(
            slots.at[g, at], slots.at[slot, at], zs_sem.at[g, m], zr_sem.at[slot, m], {"vin": chip * CORES + c}
        )

    def arrival(slot, m):
        ref = slots.at[slot, pl.ds(pl.multiple_of(m * part, 16), part)]
        return remote(ref, ref, zs_sem.at[0, 0], zr_sem.at[slot, m], partner)

    def give(i):
        at = pl.ds(pl.multiple_of(i * rows, 16), rows)
        lanes = pl.ds(pl.multiple_of((1 - c) * wide, LANES), wide)
        return remote(slots.at[n + 1, at, lanes], out.at[own_half(i)], os_sem.at[i], or_sem.at[i], partner)

    def given(i):
        at = pl.ds(pl.multiple_of(i * rows, 16), rows)
        lanes = pl.ds(pl.multiple_of(c * wide, LANES), wide)
        dst = out.at[pl.ds(pl.multiple_of((1 - c) * half + i * rows, 16), rows)]
        return remote(slots.at[n + 1, at, lanes], dst, os_sem.at[i], or_sem.at[i], partner)

    def keep(i):
        at = pl.ds(pl.multiple_of(i * rows, 16), rows)
        lanes = pl.ds(pl.multiple_of(c * wide, LANES), wide)
        return pltpu.make_async_copy(slots.at[n + 1, at, lanes], out.at[own_half(i)], ol_sem.at[i])

    def step(s, carry):
        g, i = item(s)
        slot = lax.rem(s, 2)
        if staged:
            pl.when(s == chunks)(stage_two)
            pl.when(s == (n - 1) * chunks)(stage_three)
        load(s, 0).wait()
        load(s, 1).wait()

        @pl.when(s + 1 < n * chunks)
        def _():
            @pl.when(s + 1 < chunks)
            def _():
                nxt = jnp.minimum(s + 1, chunks - 1)
                remote(
                    lent.at[pl.ds(pl.multiple_of(nxt * rows, 16), rows)],
                    lent.at[pl.ds(pl.multiple_of(nxt * rows, 16), rows)],
                    ms_sem.at[nxt], mr_sem.at[nxt], partner,
                ).wait_recv()

            load(s + 1, 0).start()
            load(s + 1, 1).start()

        def product(j, carry):
            index = jnp.where(j == 4, total + g, jnp.clip(2 * g - 1 + j, 0, total - 1))
            outside = ((j == 0) & (g == 0)) | ((j == 3) & (g == n - 1))

            @pl.when(outside)
            def _():
                sums[j] = jnp.zeros((rows, wide), jnp.float32)

            @pl.when(jnp.logical_not(outside))
            def _():
                sums[j] = jnp.dot(
                    tile[slot, 0], held[index, pl.ds(0, depth)], preferred_element_type=jnp.float32
                ) + jnp.dot(tile[slot, 1], held[index, pl.ds(depth, depth)], preferred_element_type=jnp.float32)

            return carry

        lax.fori_loop(0, 5, product, 0)

        through = ((g > k) & (k > 0)) | ((g < k) & (k < n - 1))
        into = jnp.where(g == k, n + 1, g)

        def piece(m, carry):
            at = i * pieces + m
            pl.when(through)(lambda: arrival(g, at).wait_recv())

            def block(b, carry):
                r = pl.multiple_of(m * part + b * BLOCK, BLOCK)
                whole = pl.multiple_of(i * rows + m * part + b * BLOCK, BLOCK)
                here = pl.ds(r, BLOCK)
                w = weights[pl.ds(whole, BLOCK), :]
                wxl, wxh, wyl, wyh, wzl, wzh, ws = (w[:, e : e + 1] for e in range(7))
                for t in range(2):
                    for row in range(2):
                        lanes = slice(row * LANES, (row + 1) * LANES)
                        rest = slice((1 - row) * LANES, (2 - row) * LANES)
                        value = sums[1 + t, here, lanes]
                        along = sums[1 + t, here, rest]
                        halo = sums[4, here, t * LANES : (t + 1) * LANES]
                        xl = jnp.where(lane == 0, 0.0, pltpu.roll(value, 1, 1))
                        xh = jnp.where(lane == LANES - 1, 0.0, pltpu.roll(value, LANES - 1, 1))
                        if row == 0:
                            yl, yh = jnp.where(y == 1, halo, 0.0), along
                        else:
                            yl, yh = along, jnp.where(y == 0, halo, 0.0)
                        zl, zh = sums[t, here, lanes], sums[2 + t, here, lanes]
                        flow = wxl * xl + wxh * xh + wyl * yl + wyh * yh + wzl * zl + wzh * zh
                        free = fluids[2 * g + t, :, lanes]
                        moved = value - free * (ws * value - flow)
                        there = slice((2 * t + row) * LANES, (2 * t + row + 1) * LANES)
                        before = slots[into, pl.ds(whole, BLOCK), there].astype(jnp.float32)
                        moved = moved + jnp.where(through, before, 0.0)
                        slots[into, pl.ds(whole, BLOCK), there] = moved.astype(jnp.bfloat16)
                return carry

            lax.fori_loop(0, part // BLOCK, block, 0)
            pl.when(g != k)(lambda: message(g, at).start())
            return carry

        lax.fori_loop(0, pieces, piece, 0)

        @pl.when(s >= (n - 1) * chunks)
        def _():
            def settle(m, carry):
                at = i * pieces + m
                pl.when(k > 0)(lambda: arrival(k, at).wait_recv())
                pl.when(k < n - 1)(lambda: arrival(n, at).wait_recv())

                def block(b, carry):
                    here = pl.ds(pl.multiple_of(at * part + b * BLOCK, BLOCK), BLOCK)
                    low = slots[k, here, :].astype(jnp.float32)
                    high = slots[n, here, :].astype(jnp.float32)
                    value = slots[n + 1, here, :].astype(jnp.float32)
                    value = value + jnp.where(k > 0, low, 0.0) + jnp.where(k < n - 1, high, 0.0)
                    slots[n + 1, here, :] = value.astype(jnp.bfloat16)
                    return carry

                lax.fori_loop(0, part // BLOCK, block, 0)
                return carry

            lax.fori_loop(0, pieces, settle, 0)
            keep(i).start()
            give(i).start()

        return carry

    lax.fori_loop(0, n * chunks, step, 0)

    def finish(i, carry):
        keep(i).wait()
        give(i).wait_send()
        given(i).wait_recv()
        matrix_send(i).wait_send()
        return carry

    lax.fori_loop(0, chunks, finish, 0)

    def sent(g, carry):
        @pl.when(g != k)
        def _():
            def one(m, carry):
                message(g, m).wait_send()
                return carry

            lax.fori_loop(0, chunks * pieces, one, 0)

        return carry

    lax.fori_loop(0, n, sent, 0)
    for j in range(1, total):
        flag_send(j).wait_send()
    for q in range(planes):
        core_own(q).wait_send()
        halo_send(x, q).wait_send()
        halo_pass(x * planes + q).wait_send()
        for m in range(1, groups):
            to = other_group(m)
            main_send(to, q).wait_send()
            halo_send(to, q).wait_send()
            core_pass(to * planes + q).wait_send()
            halo_pass(to * planes + q).wait_send()


def on_device(chips, groups, distribution, collision, speeds, directions, cell_flags):
    planes, depth = distribution.shape[:2]
    velocities = collision.shape[0]
    half = velocities // CORES
    rows = rows_of(half)
    pieces = 2 if rows % 32 == 0 else 1
    total = chips * CORES
    wide = 2 * LANES
    chunks = half // rows
    dist = distribution.reshape(planes, depth, wide)
    lower = jnp.where(directions == 1, speeds, 0.0)
    upper = jnp.where(directions == 1, 0.0, speeds)
    coef = jnp.stack(
        [lower[0], upper[0], lower[1], upper[1], lower[2], upper[2], speeds[0] + speeds[1] + speeds[2], speeds[0]], axis=1
    )
    fluid = jnp.broadcast_to((1 - cell_flags).astype(jnp.float32).reshape(1, wide), (BLOCK, wide))
    any_space = pl.BlockSpec(memory_space=pl.ANY)
    dma = pltpu.SemaphoreType.DMA
    size = (chips, groups, planes, depth, half, rows, pieces)
    flops = 2 * half * 2 * depth * 5 * wide * chips
    out, _ = pl.pallas_call(
        functools.partial(kernel, size),
        out_shape=(
            jax.ShapeDtypeStruct((velocities, wide), jnp.bfloat16),
            jax.ShapeDtypeStruct((half, depth), jnp.bfloat16),
        ),
        in_specs=[any_space, any_space, any_space, pl.BlockSpec(memory_space=pltpu.VMEM)],
        out_specs=(any_space, any_space),
        scratch_shapes=[
            pltpu.VMEM((total + chips, CORES * depth, wide), jnp.bfloat16),
            pltpu.VMEM((2, CORES, rows, depth), jnp.bfloat16),
            pltpu.VMEM((5, rows, wide), jnp.float32),
            pltpu.VMEM((chips + 2, half, 2 * wide), jnp.bfloat16),
            pltpu.VMEM((half, 8), jnp.float32),
            pltpu.VMEM((total, BLOCK, wide), jnp.float32),
            dma((planes + 1,)),
            dma((total,)), dma((total,)),
            dma((groups, planes)), dma((total,)),
            dma((groups, planes)), dma((total,)),
            dma((total,)), dma((total,)),
            dma((chunks,)), dma((chunks,)),
            dma((total,)), dma((total,)),
            dma((2, 2)),
            dma((chips, chunks * pieces)), dma((chips + 1, chunks * pieces)),
            dma((chunks,)), dma((chunks,)), dma((chunks,)),
        ],
        compiler_params=pltpu.CompilerParams(
            collective_id=0, has_side_effects=True, vmem_limit_bytes=60 << 20
        ),
        cost_estimate=pl.CostEstimate(flops=flops, bytes_accessed=half * depth * 4 * chips, transcendentals=0),
    )(dist, collision, coef, fluid)
    return out.reshape(1, velocities, 2, LANES)


def solution(mesh):
    return jax.shard_map(
        functools.partial(on_device, mesh.shape["vin"] // CORES, mesh.shape["vout"]),
        mesh=mesh,
        in_specs=(
            P("vout", "vin", "cell", None),
            P("vout", "vin"),
            P(None, "vout"),
            P(None, "vout"),
            P("vin", "cell", None),
        ),
        out_specs=P("vin", "vout", "cell", None),
        check_vma=False,
    )
```

```python
import functools

import jax
import jax.numpy as jnp
from jax import lax
from jax.experimental import pallas as pl
from jax.experimental.pallas import tpu as pltpu
from jax.sharding import PartitionSpec as P

MESH = pl.DeviceIdType.MESH
CORES = 2
LANES = 128
BLOCK = 16


def stripes(velocities):
    width = 2 * LANES if velocities % (2 * LANES) == 0 else LANES
    return width, pl.cdiv(velocities // width, CORES)


def kernel(
    size, dist, matrix, speeds, directions, fluid, out, lent,
    held, tile, sums, slots, flat, fluids,
    l_sem, cs_sem, cr_sem, xs_sem, xr_sem, hs_sem, hr_sem, gs_sem, gr_sem, ms_sem, mr_sem,
    fs_sem, fr_sem, t_sem, zs_sem, zr_sem, ol_sem, os_sem, or_sem,
):
    n, groups, planes, depth, width, most, least = size
    total = n * CORES
    strips = width // LANES
    wide = 2 * LANES
    vin, x, y = lax.axis_index("vin"), lax.axis_index("vout"), lax.axis_index("cell")
    k, c = vin // CORES, lax.rem(vin, CORES)
    partner = {"vin": k * CORES + 1 - c}
    chunks = jnp.where(c == 0, most, least)
    first_chunk, other_first = c * most, (1 - c) * most
    other_chunks = jnp.where(c == 0, least, most)
    mirror = 2 * x >= groups
    staged = groups == 2 and n == 4 and planes == 4

    def remote(src, dst, send, recv, where):
        return pltpu.make_async_remote_copy(
            src_ref=src, dst_ref=dst, send_sem=send, recv_sem=recv, device_id=where, device_id_type=MESH
        )

    def other_group(j):
        return lax.rem(x + j, groups)

    everyone = [{"vin": lax.rem(vin + j, total)} for j in range(1, total)]
    for j in range(groups):
        if j:
            everyone.append({"vout": other_group(j)})
        everyone.append({"vout": other_group(j), "cell": 1 - y})
    barrier = pltpu.get_barrier_semaphore()
    for where in everyone:
        pl.semaphore_signal(barrier, inc=1, device_id=where, device_id_type=MESH)
    pl.semaphore_wait(barrier, len(everyone))

    def order(t):
        at = jnp.where(mirror, n - 1 - k, k)
        usual = jnp.where(t < 2, t, n + 1 - t)
        first = jnp.where(t == 0, 1, jnp.where(t == 1, n - 1, jnp.where(t == 2, 0, n + 1 - t)))
        g = jnp.where(at == 0, first, usual)
        return jnp.where(mirror, n - 1 - g, g)

    def item(s):
        j = s - chunks
        early, late = s < chunks, s >= (n - 1) * chunks
        t = jnp.where(early, 0, jnp.where(late, n - 1, 1 + lax.rem(j, n - 2)))
        i = jnp.where(early, s, jnp.where(late, s - (n - 1) * chunks, j // (n - 2)))
        return order(t), i

    inner = pl.ds(pl.multiple_of((1 - y) * LANES, LANES), LANES)

    def main_of(p):
        return pl.ds(pl.multiple_of(p * wide, wide), wide)

    def halo_of(p):
        return pl.ds(pl.multiple_of(total * wide + p * LANES, LANES), LANES)

    def local_plane(q):
        return pltpu.make_async_copy(dist.at[q], held.at[c, main_of(x * planes + q)], l_sem.at[q])

    def core_own(q):
        p = x * planes + q
        return remote(dist.at[q], held.at[c, main_of(p)], cs_sem.at[p], cr_sem.at[p], partner)

    def core_pass(p):
        return remote(held.at[c, main_of(p)], held.at[c, main_of(p)], cs_sem.at[p], cr_sem.at[p], partner)

    def core_got(p):
        return remote(held.at[1 - c, main_of(p)], held.at[1 - c, main_of(p)], cs_sem.at[p], cr_sem.at[p], partner)

    def main_send(to, q):
        p = x * planes + q
        return remote(dist.at[q], held.at[c, main_of(p)], xs_sem.at[to, q], xr_sem.at[p], {"vout": to})

    def main_got(p):
        return remote(held.at[c, main_of(p)], held.at[c, main_of(p)], xs_sem.at[0, 0], xr_sem.at[p], {"vout": other_group(1)})

    def halo_send(to, q):
        p = x * planes + q
        return remote(
            dist.at[q, inner], held.at[c, halo_of(p)], hs_sem.at[to, q], hr_sem.at[p],
            {"vout": to, "cell": 1 - y},
        )

    def halo_got(p):
        ref = held.at[c, halo_of(p)]
        return remote(ref, ref, hs_sem.at[0, 0], hr_sem.at[p], {"cell": 1 - y})

    def halo_pass(p):
        ref = held.at[c, halo_of(p)]
        return remote(ref, ref, gs_sem.at[p], gr_sem.at[p], partner)

    def halo_end(p):
        ref = held.at[1 - c, halo_of(p)]
        return remote(ref, ref, gs_sem.at[p], gr_sem.at[p], partner)

    def lanes_of(chunk):
        return pl.ds(pl.multiple_of(chunk * width, LANES), width)

    def matrix_send(i):
        return remote(
            matrix.at[:, lanes_of(other_first + i)], lent.at[i], ms_sem.at[i], mr_sem.at[i], partner
        )

    def matrix_got(i):
        return remote(lent.at[i], lent.at[i], ms_sem.at[i], mr_sem.at[i], partner)

    def flag_send(j):
        to = lax.rem(vin + j, total)
        return remote(fluid, flat.at[vin], fs_sem.at[to], fr_sem.at[vin], {"vin": to})

    def flag_got(j):
        at = lax.rem(vin + j, total)
        return remote(fluid, flat.at[at], fs_sem.at[at], fr_sem.at[at], {"vin": at})

    def load(s, which):
        i = item(s)[1]
        slot = lax.rem(s, 2)
        if which == 0:
            src, at = matrix.at[:, lanes_of(first_chunk + i)], c
        else:
            src, at = lent.at[i], 1 - c
        return pltpu.make_async_copy(src, tile.at[slot, at], t_sem.at[slot, which])

    first_pair = lax.rem(order(0), planes // 2)

    def halo_order(j):
        if not staged:
            return j
        pair = first_pair if j < 2 else 1 - first_pair
        return pair * 2 + j % 2

    def away(to, j):
        return jnp.where(x > to, j, planes - 1 - j)

    def from_group(src, j):
        return src * planes + jnp.where(src > x, j, planes - 1 - j)

    for q in range(planes):
        core_own(q).start()
        local_plane(q).start()
    for j in range(min(2, planes)):
        halo_send(x, halo_order(j)).start()
    for m in range(1, groups):
        to = other_group(m)
        main_send(to, away(to, 0)).start()
    matrix_send(0).start()
    load(0, 0).start()
    for j in range(1, total):
        flag_send(j).start()

    def lend(i, carry):
        matrix_send(i).start()
        return carry

    lax.fori_loop(1, other_chunks, lend, 0)
    for j in range(2, planes):
        halo_send(x, halo_order(j)).start()
    for m in range(1, groups):
        to = other_group(m)
        for j in range(1, planes):
            main_send(to, away(to, j)).start()
        for j in list(range(2, planes)) + list(range(min(2, planes))):
            halo_send(to, away(to, j)).start()
    flat[vin] = fluid[...]
    matrix_got(0).wait_recv()
    load(0, 1).start()
    for j in range(1, total):
        flag_got(j).wait_recv()

    def spread(p, carry):
        for row in range(2):
            line = flat[p, 0:1, row * LANES : (row + 1) * LANES]
            fluids[p, row * LANES : (row + 1) * LANES] = jnp.broadcast_to(line, (LANES, LANES)).T
        return carry

    lax.fori_loop(0, total, spread, 0)

    own = [x * planes + halo_order(j) for j in range(planes)]

    def pass_halo(ps):
        for p in ps:
            halo_got(p).wait_recv()
            halo_pass(p).start()

    def end_halo(ps):
        for p in ps:
            halo_end(p).wait_recv()

    def pass_main(ps):
        for p in ps:
            main_got(p).wait_recv()
            core_pass(p).start()

    def end_main(ps):
        for p in ps:
            core_got(p).wait_recv()

    near = [from_group(other_group(m), 0) for m in range(1, groups)]
    far = [from_group(other_group(m), j) for m in range(1, groups) for j in range(1, planes)]
    far_halo = [from_group(other_group(m), j) for m in range(1, groups) for j in range(2, planes)]
    near_halo = [from_group(other_group(m), j) for m in range(1, groups) for j in range(min(2, planes))]

    for q in range(planes):
        local_plane(q).wait()
    end_main([x * planes + q for q in range(planes)])
    pass_halo(own[:2])
    pass_main(near)
    end_halo(own[:2])
    end_main(near)

    def stage_two():
        pass_halo(own[2:])
        pass_main(far)
        pass_halo(far_halo)
        end_halo(own[2:])
        end_main(far)
        end_halo(far_halo)

    def stage_three():
        pass_halo(near_halo)
        end_halo(near_halo)

    if not staged:
        stage_two()
        stage_three()

    near_row = lax.broadcasted_iota(jnp.int32, (BLOCK, LANES), 0)

    def message(g, i):
        up = g > k
        chip = jnp.clip(jnp.where(up, k + 1, k - 1), 0, n - 1)
        slot = jnp.where(up | (chip != g), g, n)
        return remote(
            slots.at[g, i], slots.at[slot, i], zs_sem.at[g, i], zr_sem.at[slot, i], {"vin": chip * CORES + c}
        )

    def arrival(slot, i):
        ref = slots.at[slot, i]
        return remote(ref, ref, zs_sem.at[0, 0], zr_sem.at[slot, i], partner)

    def place(chunk):
        return pl.ds(chunk * strips, strips)

    def plane_of(i, at):
        return slots.at[n + 1, i, :, pl.ds(pl.multiple_of(at * wide, wide), wide)]

    def give(i):
        return remote(
            plane_of(i, 1 - c), out.at[place(first_chunk + i)], os_sem.at[i], or_sem.at[first_chunk + i], partner
        )

    def given(i):
        dst = out.at[place(other_first + i)]
        return remote(dst, dst, os_sem.at[i], or_sem.at[other_first + i], partner)

    def keep(i):
        return pltpu.make_async_copy(plane_of(i, c), out.at[place(first_chunk + i)], ol_sem.at[i])

    def step(s, carry):
        g, i = item(s)
        slot = lax.rem(s, 2)
        if staged:
            pl.when(s == chunks)(stage_two)
            pl.when(s == (n - 1) * chunks)(stage_three)
        load(s, 0).wait()
        load(s, 1).wait()

        @pl.when(s + 1 < n * chunks)
        def _():
            @pl.when(s + 1 < chunks)
            def _():
                matrix_got(s + 1).wait_recv()

            load(s + 1, 0).start()
            load(s + 1, 1).start()

        def product(start, count, to):
            at = pl.ds(pl.multiple_of(start, wide), count)
            value = jnp.dot(held[0, at], tile[slot, 0], preferred_element_type=jnp.float32)
            value = value + jnp.dot(held[1, at], tile[slot, 1], preferred_element_type=jnp.float32)
            for q in range(strips):
                sums[q, to : to + count] = value[:, q * LANES : (q + 1) * LANES]

        @pl.when((g > 0) & (g < n - 1))
        def _():
            product((2 * g - 1) * wide, 4 * wide, 0)

        @pl.when(g == 0)
        def _():
            product(0, 3 * wide, wide)
            for q in range(strips):
                sums[q, 0:wide] = jnp.zeros((wide, LANES), jnp.float32)

        @pl.when(g == n - 1)
        def _():
            product((total - 3) * wide, 3 * wide, 0)
            for q in range(strips):
                sums[q, 3 * wide : 4 * wide] = jnp.zeros((wide, LANES), jnp.float32)

        product((total + g) * wide, wide, 4 * wide)

        through = ((g > k) & (k > 0)) | ((g < k) & (k < n - 1))
        into = jnp.where(g == k, n + 1, g)
        pl.when(through)(lambda: arrival(g, i).wait_recv())

        def move(q, carry):
            here = pl.ds(pl.multiple_of((first_chunk + i) * width + q * LANES, LANES), LANES)
            low, high = [], []
            for e in range(3):
                speed, ahead = speeds[e : e + 1, here], directions[e : e + 1, here] == 1
                low.append(jnp.broadcast_to(jnp.where(ahead, speed, 0.0), (BLOCK, LANES)))
                high.append(jnp.broadcast_to(jnp.where(ahead, 0.0, speed), (BLOCK, LANES)))
            whole = sum(low) + sum(high)
            outer_low = jnp.where(y == 1, low[1], 0.0)
            outer_high = jnp.where(y == 0, high[1], 0.0)
            for t in range(2):
                for row in range(2):
                    for b in range(LANES // BLOCK):
                        shift = b * BLOCK
                        base = (1 + t) * wide + row * LANES + shift
                        value = sums[q, base : base + BLOCK]
                        before = sums[q, base - 1 : base - 1 + BLOCK]
                        after = sums[q, base + 1 : base + 1 + BLOCK]
                        if b == 0:
                            before = jnp.where(near_row == 0, 0.0, before)
                        if shift + BLOCK == LANES:
                            after = jnp.where(near_row == BLOCK - 1, 0.0, after)
                        side = (1 + t) * wide + (1 - row) * LANES + shift
                        along = sums[q, side : side + BLOCK]
                        edge = 4 * wide + t * LANES + shift
                        halo = sums[q, edge : edge + BLOCK]
                        flow = low[0] * before + high[0] * after
                        if row == 0:
                            flow = flow + outer_low * halo + high[1] * along
                        else:
                            flow = flow + low[1] * along + outer_high * halo
                        flow = flow + low[2] * sums[q, base - wide : base - wide + BLOCK]
                        flow = flow + high[2] * sums[q, base + wide : base + wide + BLOCK]
                        free = fluids[2 * g + t, row * LANES + shift : row * LANES + shift + BLOCK]
                        moved = value - free * (whole * value - flow)
                        there = slice(base - wide, base - wide + BLOCK)
                        prior = slots[into, i, q, there].astype(jnp.float32)
                        moved = moved + jnp.where(through, prior, 0.0)
                        slots[into, i, q, there] = moved.astype(jnp.bfloat16)
            return carry

        lax.fori_loop(0, strips, move, 0)
        pl.when(g != k)(lambda: message(g, i).start())

        @pl.when(s >= (n - 1) * chunks)
        def _():
            pl.when(k > 0)(lambda: arrival(k, i).wait_recv())
            pl.when(k < n - 1)(lambda: arrival(n, i).wait_recv())

            def settle(b, carry):
                here = pl.ds(pl.multiple_of(b * 2 * BLOCK, 2 * BLOCK), 2 * BLOCK)
                for q in range(strips):
                    low = slots[k, i, q, here].astype(jnp.float32)
                    high = slots[n, i, q, here].astype(jnp.float32)
                    value = slots[n + 1, i, q, here].astype(jnp.float32)
                    value = value + jnp.where(k > 0, low, 0.0) + jnp.where(k < n - 1, high, 0.0)
                    slots[n + 1, i, q, here] = value.astype(jnp.bfloat16)
                return carry

            lax.fori_loop(0, wide // BLOCK, settle, 0)
            keep(i).start()
            give(i).start()

        return carry

    lax.fori_loop(0, n * chunks, step, 0)

    def finish(i, carry):
        keep(i).wait()
        give(i).wait_send()
        return carry

    lax.fori_loop(0, chunks, finish, 0)

    def returned(i, carry):
        given(i).wait_recv()
        matrix_send(i).wait_send()
        return carry

    lax.fori_loop(0, other_chunks, returned, 0)

    def sent(g, carry):
        @pl.when(g != k)
        def _():
            def one(m, carry):
                message(g, m).wait_send()
                return carry

            lax.fori_loop(0, chunks, one, 0)

        return carry

    lax.fori_loop(0, n, sent, 0)
    for j in range(1, total):
        flag_send(j).wait_send()
    for q in range(planes):
        core_own(q).wait_send()
        halo_send(x, q).wait_send()
        halo_pass(x * planes + q).wait_send()
        for m in range(1, groups):
            to = other_group(m)
            main_send(to, q).wait_send()
            halo_send(to, q).wait_send()
            core_pass(to * planes + q).wait_send()
            halo_pass(to * planes + q).wait_send()


def on_device(chips, groups, distribution, collision, speeds, directions, cell_flags):
    planes, depth = distribution.shape[:2]
    matrix = collision.T
    extra = -matrix.shape[1] % LANES
    if extra:
        matrix, speeds, directions = (jnp.pad(v, ((0, 0), (0, extra))) for v in (matrix, speeds, directions))
    velocities = matrix.shape[1]
    width, most = stripes(velocities)
    total = chips * CORES
    wide = 2 * LANES
    dist = distribution.transpose(0, 2, 3, 1).reshape(planes, wide, depth)
    fluid = jnp.broadcast_to((1 - cell_flags).astype(jnp.float32).reshape(1, wide), (8, wide))
    any_space = pl.BlockSpec(memory_space=pl.ANY)
    vmem = pl.BlockSpec(memory_space=pltpu.VMEM)
    dma = pltpu.SemaphoreType.DMA
    size = (chips, groups, planes, depth, width, most, velocities // width - most)
    flops = 2 * velocities * depth * 5 * wide * chips
    out, _ = pl.pallas_call(
        functools.partial(kernel, size),
        out_shape=(
            jax.ShapeDtypeStruct((velocities // LANES, wide, LANES), jnp.bfloat16),
            jax.ShapeDtypeStruct((most, depth, width), jnp.bfloat16),
        ),
        in_specs=[any_space, any_space, vmem, vmem, vmem],
        out_specs=(any_space, any_space),
        scratch_shapes=[
            pltpu.VMEM((CORES, (total + chips) * wide, depth), jnp.bfloat16),
            pltpu.VMEM((2, CORES, depth, width), jnp.bfloat16),
            pltpu.VMEM((width // LANES, 5 * wide, LANES), jnp.float32),
            pltpu.VMEM((chips + 2, most, width // LANES, 2 * wide, LANES), jnp.bfloat16),
            pltpu.VMEM((total, 8, wide), jnp.float32),
            pltpu.VMEM((total, wide, LANES), jnp.float32),
            dma((planes,)),
            dma((total,)), dma((total,)),
            dma((groups, planes)), dma((total,)),
            dma((groups, planes)), dma((total,)),
            dma((total,)), dma((total,)),
            dma((most,)), dma((most,)),
            dma((total,)), dma((total,)),
            dma((2, 2)),
            dma((chips, most)), dma((chips + 1, most)),
            dma((most,)), dma((most,)), dma((CORES * most,)),
        ],
        compiler_params=pltpu.CompilerParams(
            collective_id=0, has_side_effects=True, vmem_limit_bytes=60 << 20
        ),
        cost_estimate=pl.CostEstimate(flops=flops, bytes_accessed=velocities * depth * 2 * chips, transcendentals=0),
    )(dist, matrix, speeds, directions, fluid)
    out = out.reshape(velocities // LANES, 2, LANES, LANES).transpose(0, 3, 1, 2)
    return out.reshape(1, velocities, 2, LANES)[:, : velocities - extra]


def solution(mesh):
    return jax.shard_map(
        functools.partial(on_device, mesh.shape["vin"] // CORES, mesh.shape["vout"]),
        mesh=mesh,
        in_specs=(
            P("vout", "vin", "cell", None),
            P("vout", "vin"),
            P(None, "vout"),
            P(None, "vout"),
            P("vin", "cell", None),
        ),
        out_specs=P("vin", "vout", "cell", None),
        check_vma=False,
    )
```

```python
import functools

import jax
import jax.numpy as jnp
from jax import lax
from jax.experimental import pallas as pl
from jax.experimental.pallas import tpu as pltpu
from jax.sharding import PartitionSpec as P

MESH = pl.DeviceIdType.MESH
CORES = 2
LANES = 128
BLOCK = 16
KEPT = 2


def stripes(velocities):
    width = 2 * LANES if velocities % (2 * LANES) == 0 else LANES
    return width, pl.cdiv(velocities // width, CORES)


def kernel(
    size, dist, matrix, speeds, directions, fluid, out, lent,
    held, tile, sums, slots, flat, fluids, raw, spaced,
    l_sem, cs_sem, cr_sem, xs_sem, xr_sem, hs_sem, hr_sem, gs_sem, gr_sem, ms_sem, mr_sem,
    fs_sem, fr_sem, t_sem, zs_sem, zr_sem, ol_sem, os_sem, or_sem,
):
    n, groups, planes, depth, width, most, least = size
    total = n * CORES
    strips = width // LANES
    wide = 2 * LANES
    vin, x, y = lax.axis_index("vin"), lax.axis_index("vout"), lax.axis_index("cell")
    k, c = vin // CORES, lax.rem(vin, CORES)
    partner = {"vin": k * CORES + 1 - c}
    chunks = jnp.where(c == 0, most, least)
    first_chunk, other_first = c * most, (1 - c) * most
    other_chunks = jnp.where(c == 0, least, most)
    mirror = 2 * x >= groups
    staged = groups == 2 and n == 4 and planes == 4

    def remote(src, dst, send, recv, where):
        return pltpu.make_async_remote_copy(
            src_ref=src, dst_ref=dst, send_sem=send, recv_sem=recv, device_id=where, device_id_type=MESH
        )

    def other_group(j):
        return lax.rem(x + j, groups)

    everyone = [{"vin": lax.rem(vin + j, total)} for j in range(1, total)]
    for j in range(groups):
        if j:
            everyone.append({"vout": other_group(j)})
        everyone.append({"vout": other_group(j), "cell": 1 - y})
    barrier = pltpu.get_barrier_semaphore()
    for where in everyone:
        pl.semaphore_signal(barrier, inc=1, device_id=where, device_id_type=MESH)

    at = jnp.where(mirror, n - 1 - k, k)
    final_chip = at == n - 1

    def turned(g):
        return jnp.where(mirror, n - 1 - g, g)

    first_group = turned(jnp.where(at == 0, 1, 0)) if staged else 0
    steps = (n + 1) * chunks if staged else n * chunks
    last = steps - chunks

    def item(s):
        if not staged:
            return s // chunks, lax.rem(s, chunks)
        j = s - 2 * chunks
        third, rest = j // 3, lax.rem(j, 3)
        sent = 2 * third + rest
        length = jnp.where(at == 2, chunks, chunks - KEPT)
        one, two = sent < length, sent < length + chunks
        g = jnp.where(rest == 2, at, jnp.where(one | jnp.logical_not(two), jnp.where(at == 2, 1, 2), 3))
        i = jnp.where(rest == 2, third, jnp.where(one, sent, jnp.where(two, sent - length, sent - chunks)))
        g = jnp.where(final_chip, 1 + j // chunks, g)
        i = jnp.where(final_chip, lax.rem(s, chunks), i)
        early = j < 0
        return jnp.where(early, first_group, turned(g)), jnp.where(early, lax.rem(s, chunks), i)

    inner, outer = 1 - y, y

    def inner_of(p):
        return pl.ds(pl.multiple_of(p * wide + inner * LANES, LANES), LANES)

    diagonal = lax.broadcasted_iota(jnp.int32, (LANES, LANES), 0) == lax.broadcasted_iota(jnp.int32, (LANES, LANES), 1)
    unit = jnp.where(diagonal, 1.0, 0.0).astype(jnp.bfloat16)

    def flipped(values):
        exact = lax.dot_general(unit, values, (((1,), (1,)), ((), ())), preferred_element_type=jnp.float32)
        return exact.astype(jnp.bfloat16)

    def main_of(p):
        return pl.ds(pl.multiple_of(p * wide, wide), wide)

    def halo_of(p):
        return pl.ds(pl.multiple_of(total * wide + p * LANES, LANES), LANES)

    def fetch(q):
        return pltpu.make_async_copy(dist.at[q], raw.at[q % 2], l_sem.at[q])

    def turn(q):
        spaced[...] = raw[q % 2].astype(jnp.float32)
        for row in range(2):
            values = spaced[pl.ds(row, depth, stride=2), :].astype(jnp.bfloat16)
            at = pl.ds(pl.multiple_of((x * planes + q) * wide + row * LANES, LANES), LANES)
            held[c, at] = flipped(values)

    def core_own(q):
        return core_pass(x * planes + q)

    def core_pass(p):
        return remote(held.at[c, main_of(p)], held.at[c, main_of(p)], cs_sem.at[p], cr_sem.at[p], partner)

    def core_got(p):
        return remote(held.at[1 - c, main_of(p)], held.at[1 - c, main_of(p)], cs_sem.at[p], cr_sem.at[p], partner)

    def main_send(to, q):
        p = x * planes + q
        return remote(held.at[c, main_of(p)], held.at[c, main_of(p)], xs_sem.at[to, q], xr_sem.at[p], {"vout": to})

    def main_got(p):
        return remote(held.at[c, main_of(p)], held.at[c, main_of(p)], xs_sem.at[0, 0], xr_sem.at[p], {"vout": other_group(1)})

    def halo_send(to, q):
        p = x * planes + q
        return remote(
            held.at[c, inner_of(p)], held.at[c, halo_of(p)], hs_sem.at[to, q], hr_sem.at[p],
            {"vout": to, "cell": 1 - y},
        )

    def halo_got(p):
        ref = held.at[c, halo_of(p)]
        return remote(ref, ref, hs_sem.at[0, 0], hr_sem.at[p], {"cell": 1 - y})

    def halo_pass(p):
        ref = held.at[c, halo_of(p)]
        return remote(ref, ref, gs_sem.at[p], gr_sem.at[p], partner)

    def halo_end(p):
        ref = held.at[1 - c, halo_of(p)]
        return remote(ref, ref, gs_sem.at[p], gr_sem.at[p], partner)

    def lanes_of(chunk):
        return pl.ds(pl.multiple_of(chunk * width, LANES), width)

    def matrix_send(i):
        return remote(
            matrix.at[:, lanes_of(other_first + i)], lent.at[i], ms_sem.at[i], mr_sem.at[i], partner
        )

    def matrix_got(i):
        return remote(lent.at[i], lent.at[i], ms_sem.at[i], mr_sem.at[i], partner)

    def flag_send(j):
        to = lax.rem(vin + j, total)
        return remote(fluid, flat.at[vin], fs_sem.at[to], fr_sem.at[vin], {"vin": to})

    def flag_got(j):
        at = lax.rem(vin + j, total)
        return remote(fluid, flat.at[at], fs_sem.at[at], fr_sem.at[at], {"vin": at})

    def load(s, which):
        i = item(s)[1]
        slot = lax.rem(s, 2)
        if which == 0:
            src, at = matrix.at[:, lanes_of(first_chunk + i)], c
        else:
            src, at = lent.at[i], 1 - c
        return pltpu.make_async_copy(src, tile.at[slot, at], t_sem.at[slot, which])

    first_pair = lax.rem(first_group, planes // 2)

    def halo_order(j):
        if not staged:
            return j
        pair = first_pair if j < 2 else 1 - first_pair
        return pair * 2 + j % 2

    def away(to, j):
        return jnp.where(x > to, j, planes - 1 - j)

    def from_group(src, j):
        return src * planes + jnp.where(src > x, j, planes - 1 - j)

    load(0, 0).start()
    for q in range(min(2, planes)):
        fetch(q).start()
    for q in range(planes):
        fetch(q).wait()
        turn(q)
        if q + 2 < planes:
            fetch(q + 2).start()
        if q == 0:
            pl.semaphore_wait(barrier, len(everyone))
            matrix_send(0).start()
        core_own(q).start()
    for j in range(min(2, planes)):
        halo_send(x, halo_order(j)).start()
    for m in range(1, groups):
        to = other_group(m)
        main_send(to, away(to, 0)).start()
    for j in range(1, total):
        flag_send(j).start()

    def lend(i, carry):
        matrix_send(i).start()
        return carry

    lax.fori_loop(1, other_chunks, lend, 0)
    for j in range(2, planes):
        halo_send(x, halo_order(j)).start()
    for m in range(1, groups):
        to = other_group(m)
        for j in range(1, min(3, planes)):
            main_send(to, away(to, j)).start()
        for j in range(min(2, planes)):
            halo_send(to, away(to, j)).start()
        for j in range(3, planes):
            main_send(to, away(to, j)).start()
        for j in range(2, planes):
            halo_send(to, away(to, j)).start()
    flat[vin] = fluid[...]
    for q in range(strips):
        sums[q, 4 * wide : 5 * wide] = jnp.zeros((wide, LANES), jnp.float32)
    matrix_got(0).wait_recv()
    load(0, 1).start()
    for j in range(1, total):
        flag_got(j).wait_recv()

    def spread(p, carry):
        for row in range(2):
            line = flat[p, 0:1, row * LANES : (row + 1) * LANES]
            fluids[p, row * LANES : (row + 1) * LANES] = jnp.broadcast_to(line, (LANES, LANES)).T
        return carry

    lax.fori_loop(0, total, spread, 0)

    own = [x * planes + halo_order(j) for j in range(planes)]

    def pass_halo(ps):
        for p in ps:
            halo_got(p).wait_recv()
            halo_pass(p).start()

    def end_halo(ps):
        for p in ps:
            halo_end(p).wait_recv()

    def pass_main(ps):
        for p in ps:
            main_got(p).wait_recv()
            core_pass(p).start()

    def end_main(ps):
        for p in ps:
            core_got(p).wait_recv()

    def others(low, high):
        return [from_group(other_group(m), j) for m in range(1, groups) for j in range(low, min(high, planes))]

    near, middle, far, near_halo, far_halo = others(0, 1), others(1, 3), others(3, 99), others(0, 2), others(2, 99)
    end_main([x * planes + q for q in range(planes)])

    def at_step(s):
        def when(step, *calls):
            @pl.when(s == step)
            def _():
                for call, ps in calls:
                    call(ps)

        when(chunks - 4, (pass_halo, own[:2]), (pass_main, near))
        when(chunks, (end_halo, own[:2]), (end_main, near))
        when(2 * chunks - 3, (pass_halo, own[2:]), (pass_main, middle))
        when(2 * chunks, (end_halo, own[2:]))
        when(2 * chunks - 1, (pass_halo, near_halo))
        when(jnp.where(final_chip, 3 * chunks, 2 * chunks), (end_main, middle), (end_halo, near_halo))
        when(2 * chunks + 12, (pass_main, far), (pass_halo, far_halo))
        when(2 * chunks + 15, (end_main, far), (end_halo, far_halo))

    if not staged:
        pass_halo(own)
        pass_main(near + middle + far)
        pass_halo(near_halo + far_halo)
        end_halo(own)
        end_main(near + middle + far)
        end_halo(near_halo + far_halo)

    near_row = lax.broadcasted_iota(jnp.int32, (BLOCK, LANES), 0)

    parts = (pl.ds(0, LANES), pl.ds(LANES, 3 * LANES))

    def message(g, i, part):
        up = g > k
        chip = jnp.clip(jnp.where(up, k + 1, k - 1), 0, n - 1)
        slot = jnp.where(up | (chip != g), g, n)
        rows = parts[part]
        return remote(
            slots.at[g, i, :, rows], slots.at[slot, i, :, rows], zs_sem.at[part, g, i], zr_sem.at[part, slot, i],
            {"vin": chip * CORES + c},
        )

    def arrival(slot, i, part):
        ref = slots.at[slot, i, :, parts[part]]
        return remote(ref, ref, zs_sem.at[0, 0, 0], zr_sem.at[part, slot, i], partner)

    first_plane = jnp.where(mirror, 1, 0)

    def spot(t, row):
        return jnp.where(first_plane == t, 0, 2) + jnp.where(outer == row, 0, 1)

    def place(chunk):
        return pl.ds(chunk * strips, strips)

    def plane_of(i, at):
        return slots.at[n + 1, i, :, pl.ds(pl.multiple_of(at * wide, wide), wide)]

    def give(i):
        return remote(
            plane_of(i, 1 - c), out.at[place(first_chunk + i)], os_sem.at[i], or_sem.at[first_chunk + i], partner
        )

    def given(i):
        dst = out.at[place(other_first + i)]
        return remote(dst, dst, os_sem.at[i], or_sem.at[other_first + i], partner)

    def keep(i):
        return pltpu.make_async_copy(plane_of(i, c), out.at[place(first_chunk + i)], ol_sem.at[i])

    def step(s, carry):
        g, i = item(s)
        slot = lax.rem(s, 2)
        if staged:
            at_step(s)
        load(s, 0).wait()
        load(s, 1).wait()

        @pl.when(s + 1 < steps)
        def _():
            @pl.when(s + 1 < chunks)
            def _():
                matrix_got(s + 1).wait_recv()

            load(s + 1, 0).start()
            load(s + 1, 1).start()

        def product(start, count, to):
            at = pl.ds(pl.multiple_of(start, wide), count)
            value = jnp.dot(held[0, at], tile[slot, 0], preferred_element_type=jnp.float32)
            value = value + jnp.dot(held[1, at], tile[slot, 1], preferred_element_type=jnp.float32)
            for q in range(strips):
                sums[q, to : to + count] = value[:, q * LANES : (q + 1) * LANES]

        def clear(at):
            for q in range(strips):
                sums[q, at : at + wide] = jnp.zeros((wide, LANES), jnp.float32)

        full = s >= chunks if staged else s >= 0

        @pl.when(full)
        def _():
            @pl.when((g > 0) & (g < n - 1))
            def _():
                product((2 * g - 1) * wide, 4 * wide, 0)

            @pl.when(g == 0)
            def _():
                product(0, 3 * wide, wide)
                clear(0)

            @pl.when(g == n - 1)
            def _():
                product((total - 3) * wide, 3 * wide, 0)
                clear(3 * wide)

            product((total + g) * wide, wide, 4 * wide)

        if staged:

            @pl.when(jnp.logical_not(full))
            def _():
                @pl.when(jnp.logical_not(mirror) & (g > 0))
                def _():
                    product((2 * g - 1) * wide, 3 * wide, 0)

                @pl.when(jnp.logical_not(mirror) & (g == 0))
                def _():
                    product(0, 2 * wide, wide)
                    clear(0)

                @pl.when(mirror & (g < n - 1))
                def _():
                    product(2 * g * wide, 3 * wide, wide)

                @pl.when(mirror & (g == n - 1))
                def _():
                    product(2 * g * wide, 2 * wide, wide)
                    clear(3 * wide)

        through = ((g > k) & (k > 0)) | ((g < k) & (k < n - 1))
        into = jnp.where(g == k, n + 1, g)
        if staged:
            does = (s < chunks) | (s >= 2 * chunks), s >= chunks
        else:
            does = s >= 0, s >= 0
        for part in range(2):
            pl.when(through & does[part])(lambda: arrival(g, i, part).wait_recv())

        def move(q, carry):
            here = pl.ds(pl.multiple_of((first_chunk + i) * width + q * LANES, LANES), LANES)
            low, high = [], []
            for e in range(3):
                speed, ahead = speeds[e : e + 1, here], directions[e : e + 1, here] == 1
                low.append(jnp.broadcast_to(jnp.where(ahead, speed, 0.0), (BLOCK, LANES)))
                high.append(jnp.broadcast_to(jnp.where(ahead, 0.0, speed), (BLOCK, LANES)))
            whole = sum(low) + sum(high)
            outer_low = jnp.where(y == 1, low[1], 0.0)
            outer_high = jnp.where(y == 0, high[1], 0.0)
            def quarter(t, row):
                at = spot(t, row)

                @pl.when(((at == 0) & does[0]) | ((at > 0) & does[1]))
                def _():
                    for b in range(LANES // BLOCK):
                        shift = b * BLOCK
                        base = (1 + t) * wide + row * LANES + shift
                        value = sums[q, base : base + BLOCK]
                        before = sums[q, base - 1 : base - 1 + BLOCK]
                        after = sums[q, base + 1 : base + 1 + BLOCK]
                        if b == 0:
                            before = jnp.where(near_row == 0, 0.0, before)
                        if shift + BLOCK == LANES:
                            after = jnp.where(near_row == BLOCK - 1, 0.0, after)
                        side = (1 + t) * wide + (1 - row) * LANES + shift
                        along = sums[q, side : side + BLOCK]
                        edge = 4 * wide + t * LANES + shift
                        halo = sums[q, edge : edge + BLOCK]
                        flow = low[0] * before + high[0] * after
                        if row == 0:
                            flow = flow + outer_low * halo + high[1] * along
                        else:
                            flow = flow + low[1] * along + outer_high * halo
                        flow = flow + low[2] * sums[q, base - wide : base - wide + BLOCK]
                        flow = flow + high[2] * sums[q, base + wide : base + wide + BLOCK]
                        free = fluids[2 * g + t, row * LANES + shift : row * LANES + shift + BLOCK]
                        moved = value - free * (whole * value - flow)
                        there = pl.ds(pl.multiple_of(at * LANES + shift, BLOCK), BLOCK)
                        prior = slots[into, i, q, there].astype(jnp.float32)
                        moved = moved + jnp.where(through, prior, 0.0)
                        slots[into, i, q, there] = moved.astype(jnp.bfloat16)

            for t in range(2):
                for row in range(2):
                    quarter(t, row)
            return carry

        lax.fori_loop(0, strips, move, 0)
        for part in range(2):
            pl.when((g != k) & does[part])(lambda: message(g, i, part).start())

        f = s - last

        @pl.when((f >= 0) & (f < chunks))
        def _():
            for part in range(2):
                pl.when(k > 0)(lambda: arrival(k, f, part).wait_recv())
                pl.when(k < n - 1)(lambda: arrival(n, f, part).wait_recv())

            def settle(q, carry):
                for t in range(2):
                    for row in range(2):
                        here = pl.ds(pl.multiple_of(spot(t, row) * LANES, LANES), LANES)
                        low = slots[k, f, q, here].astype(jnp.float32)
                        high = slots[n, f, q, here].astype(jnp.float32)
                        value = slots[n + 1, f, q, here].astype(jnp.float32)
                        value = value + jnp.where(k > 0, low, 0.0) + jnp.where(k < n - 1, high, 0.0)
                        exact = lax.dot_general(
                            unit, value.astype(jnp.bfloat16), (((1,), (1,)), ((), ())),
                            preferred_element_type=jnp.float32,
                        )
                        spaced[pl.ds(t * wide + row, LANES, stride=2), :] = exact
                slots[n + 1, f, q] = spaced[pl.ds(0, 2 * wide), :].astype(jnp.bfloat16)
                return carry

            lax.fori_loop(0, strips, settle, 0)
            keep(f).start()
            give(f).start()

        return carry

    lax.fori_loop(0, steps, step, 0)

    def finish(i, carry):
        keep(i).wait()
        give(i).wait_send()
        return carry

    lax.fori_loop(0, chunks, finish, 0)

    def returned(i, carry):
        given(i).wait_recv()
        matrix_send(i).wait_send()
        return carry

    lax.fori_loop(0, other_chunks, returned, 0)

    def sent(g, carry):
        @pl.when(g != k)
        def _():
            def one(m, carry):
                message(g, m, 0).wait_send()
                message(g, m, 1).wait_send()
                return carry

            lax.fori_loop(0, chunks, one, 0)

        return carry

    lax.fori_loop(0, n, sent, 0)
    for j in range(1, total):
        flag_send(j).wait_send()
    for q in range(planes):
        core_own(q).wait_send()
        halo_send(x, q).wait_send()
        halo_pass(x * planes + q).wait_send()
        for m in range(1, groups):
            to = other_group(m)
            main_send(to, q).wait_send()
            halo_send(to, q).wait_send()
            core_pass(to * planes + q).wait_send()
            halo_pass(to * planes + q).wait_send()


def on_device(chips, groups, distribution, collision, speeds, directions, cell_flags):
    planes, depth = distribution.shape[:2]
    matrix = collision.T
    extra = -matrix.shape[1] % LANES
    if extra:
        matrix, speeds, directions = (jnp.pad(v, ((0, 0), (0, extra))) for v in (matrix, speeds, directions))
    velocities = matrix.shape[1]
    width, most = stripes(velocities)
    total = chips * CORES
    wide = 2 * LANES
    dist = distribution.reshape(planes, 2 * depth, LANES)
    fluid = jnp.broadcast_to((1 - cell_flags).astype(jnp.float32).reshape(1, wide), (8, wide))
    any_space = pl.BlockSpec(memory_space=pl.ANY)
    vmem = pl.BlockSpec(memory_space=pltpu.VMEM)
    dma = pltpu.SemaphoreType.DMA
    size = (chips, groups, planes, depth, width, most, velocities // width - most)
    flops = 2 * velocities * depth * 5 * wide * chips
    out, _ = pl.pallas_call(
        functools.partial(kernel, size),
        out_shape=(
            jax.ShapeDtypeStruct((velocities // LANES, wide, LANES), jnp.bfloat16),
            jax.ShapeDtypeStruct((most, depth, width), jnp.bfloat16),
        ),
        in_specs=[any_space, any_space, vmem, vmem, vmem],
        out_specs=(any_space, any_space),
        scratch_shapes=[
            pltpu.VMEM((CORES, (total + chips) * wide, depth), jnp.bfloat16),
            pltpu.VMEM((2, CORES, depth, width), jnp.bfloat16),
            pltpu.VMEM((width // LANES, 5 * wide, LANES), jnp.float32),
            pltpu.VMEM((chips + 2, most, width // LANES, 2 * wide, LANES), jnp.bfloat16),
            pltpu.VMEM((total, 8, wide), jnp.float32),
            pltpu.VMEM((total, wide, LANES), jnp.float32),
            pltpu.VMEM((2, 2 * depth, LANES), jnp.bfloat16),
            pltpu.VMEM((2 * depth, LANES), jnp.float32),
            dma((planes,)),
            dma((total,)), dma((total,)),
            dma((groups, planes)), dma((total,)),
            dma((groups, planes)), dma((total,)),
            dma((total,)), dma((total,)),
            dma((most,)), dma((most,)),
            dma((total,)), dma((total,)),
            dma((2, 2)),
            dma((2, chips, most)), dma((2, chips + 1, most)),
            dma((most,)), dma((most,)), dma((CORES * most,)),
        ],
        compiler_params=pltpu.CompilerParams(
            collective_id=0, has_side_effects=True, vmem_limit_bytes=60 << 20
        ),
        cost_estimate=pl.CostEstimate(flops=flops, bytes_accessed=velocities * depth * 2 * chips, transcendentals=0),
    )(dist, matrix, speeds, directions, fluid)
    return out.reshape(1, velocities, 2, LANES)[:, : velocities - extra]


def solution(mesh):
    return jax.shard_map(
        functools.partial(on_device, mesh.shape["vin"] // CORES, mesh.shape["vout"]),
        mesh=mesh,
        in_specs=(
            P("vout", "vin", "cell", None),
            P("vout", "vin"),
            P(None, "vout"),
            P(None, "vout"),
            P("vin", "cell", None),
        ),
        out_specs=P("vin", "vout", "cell", None),
        check_vma=False,
    )
```

```python
import functools

import jax
import jax.numpy as jnp
from jax import lax
from jax.experimental import pallas as pl
from jax.experimental.pallas import tpu as pltpu
from jax.sharding import PartitionSpec as P

MESH = pl.DeviceIdType.MESH
CORES = 2
LANES = 128
BLOCK = 16
KEPT = 3
AHEAD = 8


def stripes(velocities):
    width = 2 * LANES if velocities % (2 * LANES) == 0 else LANES
    return width, pl.cdiv(velocities // width, CORES)


def kernel(
    size, dist, matrix, speeds, directions, fluid, out, lent,
    held, tile, sums, slots, flat, fluids, raw, spaced,
    l_sem, cs_sem, cr_sem, xs_sem, xr_sem, hs_sem, hr_sem, gs_sem, gr_sem, ms_sem, mr_sem,
    fs_sem, fr_sem, t_sem, zs_sem, zr_sem, ol_sem, os_sem, or_sem,
):
    n, groups, planes, depth, width, most, least = size
    total = n * CORES
    strips = width // LANES
    wide = 2 * LANES
    vin, x, y = lax.axis_index("vin"), lax.axis_index("vout"), lax.axis_index("cell")
    k, c = vin // CORES, lax.rem(vin, CORES)
    partner = {"vin": k * CORES + 1 - c}
    chunks = jnp.where(c == 0, most, least)
    first_chunk, other_first = c * most, (1 - c) * most
    other_chunks = jnp.where(c == 0, least, most)
    mirror = 2 * x >= groups
    staged = groups == 2 and n == 4 and planes == 4

    def remote(src, dst, send, recv, where):
        return pltpu.make_async_remote_copy(
            src_ref=src, dst_ref=dst, send_sem=send, recv_sem=recv, device_id=where, device_id_type=MESH
        )

    def other_group(j):
        return lax.rem(x + j, groups)

    everyone = [{"vin": lax.rem(vin + j, total)} for j in range(1, total)]
    for j in range(groups):
        if j:
            everyone.append({"vout": other_group(j)})
        everyone.append({"vout": other_group(j), "cell": 1 - y})
    barrier = pltpu.get_barrier_semaphore()
    for where in everyone:
        pl.semaphore_signal(barrier, inc=1, device_id=where, device_id_type=MESH)

    at = jnp.where(mirror, n - 1 - k, k)
    final_chip = at == n - 1

    def turned(g):
        return jnp.where(mirror, n - 1 - g, g)

    first_group = turned(jnp.where(at <= 1, 1, 0)) if staged else 0
    steps = n * chunks + AHEAD if staged else n * chunks
    last = steps - chunks

    held_back = jnp.where(at == 0, KEPT, 0)
    share = jnp.where(at == 0, 10, 12)
    between = at == 1 if staged else False
    begin = jnp.where(between, AHEAD, 0)

    def item(s):
        if not staged:
            return s // chunks, lax.rem(s, chunks)
        j = s - AHEAD - chunks + held_back
        done = jnp.minimum(share * j // 30, chunks)
        alone = jnp.minimum(share * (j + 1) // 30, chunks) > done
        sent = j - done
        one, over = sent < chunks, sent >= 2 * chunks
        g = jnp.where(one, jnp.where(at == 2, 1, 2), jnp.where(over, 1, 3))
        i = jnp.where(one, sent, jnp.where(over, sent - chunks - KEPT, sent - chunks))
        g = jnp.where(alone, jnp.where(at == 1, 0, at), g)
        i = jnp.where(alone, done, i)
        g = jnp.where(final_chip, 1 + j // chunks, g)
        i = jnp.where(final_chip, lax.rem(j, chunks), i)
        early = j < 0
        return jnp.where(early, first_group, turned(g)), jnp.where(early, jnp.where(s < AHEAD, s, s - AHEAD), i)

    inner, outer = 1 - y, y

    def inner_of(p):
        return pl.ds(pl.multiple_of(p * wide + inner * LANES, LANES), LANES)

    diagonal = lax.broadcasted_iota(jnp.int32, (LANES, LANES), 0) == lax.broadcasted_iota(jnp.int32, (LANES, LANES), 1)
    unit = jnp.where(diagonal, 1.0, 0.0).astype(jnp.bfloat16)

    def flipped(values):
        exact = lax.dot_general(unit, values, (((1,), (1,)), ((), ())), preferred_element_type=jnp.float32)
        return exact.astype(jnp.bfloat16)

    def main_of(p):
        return pl.ds(pl.multiple_of(p * wide, wide), wide)

    def halo_of(p):
        return pl.ds(pl.multiple_of(total * wide + p * LANES, LANES), LANES)

    first_pair = lax.rem(first_group, planes // 2)

    def halo_order(j):
        if not staged:
            return j
        pair = first_pair if j < 2 else 1 - first_pair
        return pair * 2 + j % 2

    def fetch(j):
        return pltpu.make_async_copy(dist.at[halo_order(j)], raw.at[j % 2], l_sem.at[j])

    def turn(j):
        q = halo_order(j)
        spaced[...] = raw[j % 2].astype(jnp.float32)
        for row in range(2):
            values = spaced[pl.ds(row, depth, stride=2), :].astype(jnp.bfloat16)
            at = pl.ds(pl.multiple_of((x * planes + q) * wide + row * LANES, LANES), LANES)
            held[c, at] = flipped(values)

    def core_own(q):
        return core_pass(x * planes + q)

    def core_pass(p):
        return remote(held.at[c, main_of(p)], held.at[c, main_of(p)], cs_sem.at[p], cr_sem.at[p], partner)

    def core_got(p):
        return remote(held.at[1 - c, main_of(p)], held.at[1 - c, main_of(p)], cs_sem.at[p], cr_sem.at[p], partner)

    def main_send(to, q):
        p = x * planes + q
        return remote(held.at[c, main_of(p)], held.at[c, main_of(p)], xs_sem.at[to, q], xr_sem.at[p], {"vout": to})

    def main_got(p):
        return remote(held.at[c, main_of(p)], held.at[c, main_of(p)], xs_sem.at[0, 0], xr_sem.at[p], {"vout": other_group(1)})

    def halo_send(to, q):
        p = x * planes + q
        return remote(
            held.at[c, inner_of(p)], held.at[c, halo_of(p)], hs_sem.at[to, q], hr_sem.at[p],
            {"vout": to, "cell": 1 - y},
        )

    def relay(p):
        to, q = p // planes, planes - 1 - lax.rem(p, planes)
        return remote(
            held.at[c, inner_of(p)], held.at[c, halo_of(p)], hs_sem.at[to, q], hr_sem.at[p], {"cell": 1 - y}
        )

    def halo_got(p):
        ref = held.at[c, halo_of(p)]
        return remote(ref, ref, hs_sem.at[0, 0], hr_sem.at[p], {"cell": 1 - y})

    def halo_pass(p):
        ref = held.at[c, halo_of(p)]
        return remote(ref, ref, gs_sem.at[p], gr_sem.at[p], partner)

    def halo_end(p):
        ref = held.at[1 - c, halo_of(p)]
        return remote(ref, ref, gs_sem.at[p], gr_sem.at[p], partner)

    def lanes_of(chunk):
        return pl.ds(pl.multiple_of(chunk * width, LANES), width)

    def matrix_send(i):
        return remote(
            matrix.at[:, lanes_of(other_first + i)], lent.at[i], ms_sem.at[i], mr_sem.at[i], partner
        )

    def matrix_got(i):
        return remote(lent.at[i], lent.at[i], ms_sem.at[i], mr_sem.at[i], partner)

    def flag_send(j):
        to = lax.rem(vin + j, total)
        return remote(fluid, flat.at[vin], fs_sem.at[to], fr_sem.at[vin], {"vin": to})

    def flag_got(j):
        at = lax.rem(vin + j, total)
        return remote(fluid, flat.at[at], fs_sem.at[at], fr_sem.at[at], {"vin": at})

    def load(s, which):
        i = item(s)[1]
        slot = lax.rem(s, 2)
        if which == 0:
            src, at = matrix.at[:, lanes_of(first_chunk + i)], c
        else:
            src, at = lent.at[i], 1 - c
        return pltpu.make_async_copy(src, tile.at[slot, at], t_sem.at[slot, which])

    def away(to, j):
        return jnp.where(x > to, j, planes - 1 - j)

    def from_group(src, j):
        return src * planes + jnp.where(src > x, j, planes - 1 - j)

    load(begin, 0).start()
    for j in range(min(2, planes)):
        fetch(j).start()
    for j in range(planes):
        fetch(j).wait()
        turn(j)
        if j + 2 < planes:
            fetch(j + 2).start()
        if j == 0:
            pl.semaphore_wait(barrier, len(everyone))
            matrix_send(0).start()
        core_own(halo_order(j)).start()
        if j < 2:
            halo_send(x, halo_order(j)).start()
    for m in range(1, groups):
        to = other_group(m)
        main_send(to, away(to, 0)).start()
    for j in range(1, total):
        flag_send(j).start()

    def lend(i, carry):
        matrix_send(i).start()
        return carry

    lax.fori_loop(1, other_chunks, lend, 0)
    for j in range(2, planes):
        halo_send(x, halo_order(j)).start()
    for m in range(1, groups):
        to = other_group(m)
        for j in range(1, min(3, planes)):
            main_send(to, away(to, j)).start()
        if not staged:
            for j in range(min(2, planes)):
                halo_send(to, away(to, j)).start()
        for j in range(3, planes):
            main_send(to, away(to, j)).start()
        for j in range(2, planes):
            halo_send(to, away(to, j)).start()
    flat[vin] = fluid[...]
    for q in range(strips):
        sums[q, 4 * wide : 5 * wide] = jnp.zeros((wide, LANES), jnp.float32)
    matrix_got(0).wait_recv()
    load(begin, 1).start()
    for j in range(1, total):
        flag_got(j).wait_recv()

    def spread(p, carry):
        for row in range(2):
            line = flat[p, 0:1, row * LANES : (row + 1) * LANES]
            fluids[p, row * LANES : (row + 1) * LANES] = jnp.broadcast_to(line, (LANES, LANES)).T
        return carry

    lax.fori_loop(0, total, spread, 0)

    own = [x * planes + halo_order(j) for j in range(planes)]

    def pass_halo(ps):
        for p in ps:
            halo_got(p).wait_recv()
            halo_pass(p).start()

    def end_halo(ps):
        for p in ps:
            halo_end(p).wait_recv()

    def pass_main(ps):
        for p in ps:
            main_got(p).wait_recv()
            core_pass(p).start()

    def relay_rows(ps):
        for p in ps:
            relay(p).start()

    def end_main(ps):
        for p in ps:
            core_got(p).wait_recv()

    def others(low, high):
        return [from_group(other_group(m), j) for m in range(1, groups) for j in range(low, min(high, planes))]

    near, middle, far, near_halo, far_halo = others(0, 1), others(1, 3), others(3, 99), others(0, 2), others(2, 99)
    end_main([x * planes + q for q in range(planes)])

    def at_step(s):
        def when(step, *calls):
            @pl.when(s == step)
            def _():
                for call, ps in calls:
                    call(ps)

        when(jnp.where(between, AHEAD, AHEAD - 2), (pass_halo, own[:2]), (pass_main, near), (relay_rows, near))
        when(AHEAD, (end_halo, own[:2]), (end_main, near))
        when(AHEAD + 7, (pass_main, middle[:1]), (relay_rows, middle[:1]))
        when(AHEAD + chunks - KEPT - 2, (pass_halo, own[2:]), (pass_main, middle[1:]), (pass_halo, near_halo))
        when(AHEAD + chunks - KEPT, (end_halo, own[2:]))
        when(
            jnp.where(final_chip, AHEAD + 2 * chunks, AHEAD + chunks - KEPT), (end_main, middle), (end_halo, near_halo)
        )
        when(AHEAD + chunks + 12, (pass_main, far), (pass_halo, far_halo))
        when(AHEAD + chunks + 15, (end_main, far), (end_halo, far_halo))

    if not staged:
        pass_halo(own)
        pass_main(near + middle + far)
        pass_halo(near_halo + far_halo)
        end_halo(own)
        end_main(near + middle + far)
        end_halo(near_halo + far_halo)

    near_row = lax.broadcasted_iota(jnp.int32, (BLOCK, LANES), 0)

    parts = (pl.ds(0, LANES), pl.ds(LANES, 3 * LANES))

    def message(g, i, part):
        up = g > k
        chip = jnp.clip(jnp.where(up, k + 1, k - 1), 0, n - 1)
        slot = jnp.where(up | (chip != g), g, n)
        rows = parts[part]
        return remote(
            slots.at[g, i, :, rows], slots.at[slot, i, :, rows], zs_sem.at[part, g, i], zr_sem.at[part, slot, i],
            {"vin": chip * CORES + c},
        )

    def arrival(slot, i, part):
        ref = slots.at[slot, i, :, parts[part]]
        return remote(ref, ref, zs_sem.at[0, 0, 0], zr_sem.at[part, slot, i], partner)

    first_plane = jnp.where(mirror, 1, 0)

    def spot(t, row):
        return jnp.where(first_plane == t, 0, 2) + jnp.where(outer == row, 0, 1)

    def place(chunk):
        return pl.ds(chunk * strips, strips)

    def plane_of(i, at):
        return slots.at[n + 1, i, :, pl.ds(pl.multiple_of(at * wide, wide), wide)]

    def give(i):
        return remote(
            plane_of(i, 1 - c), out.at[place(first_chunk + i)], os_sem.at[i], or_sem.at[first_chunk + i], partner
        )

    def given(i):
        dst = out.at[place(other_first + i)]
        return remote(dst, dst, os_sem.at[i], or_sem.at[other_first + i], partner)

    def keep(i):
        return pltpu.make_async_copy(plane_of(i, c), out.at[place(first_chunk + i)], ol_sem.at[i])

    def step(s, carry):
        g, i = item(s)
        slot = lax.rem(s, 2)
        if staged:
            at_step(s)
        load(s, 0).wait()
        load(s, 1).wait()

        @pl.when(s + 1 < steps)
        def _():
            if staged:
                later = s + 1 - AHEAD
                first_use = jnp.where(between, 1, AHEAD)
                pl.when(later < 0)(lambda: matrix_got(s + 1).wait_recv())
                pl.when((later >= first_use) & (later < chunks - KEPT))(lambda: matrix_got(later).wait_recv())

                @pl.when(later == chunks - KEPT)
                def _():
                    for e in range(KEPT):
                        matrix_got(chunks - KEPT + e).wait_recv()

            else:
                pl.when(s + 1 < chunks)(lambda: matrix_got(s + 1).wait_recv())

            load(s + 1, 0).start()
            load(s + 1, 1).start()

        def product(start, count, to):
            at = pl.ds(pl.multiple_of(start, wide), count)
            value = jnp.dot(held[0, at], tile[slot, 0], preferred_element_type=jnp.float32)
            value = value + jnp.dot(held[1, at], tile[slot, 1], preferred_element_type=jnp.float32)
            for q in range(strips):
                sums[q, to : to + count] = value[:, q * LANES : (q + 1) * LANES]

        def clear(at):
            for q in range(strips):
                sums[q, at : at + wide] = jnp.zeros((wide, LANES), jnp.float32)

        full = s >= AHEAD if staged else s >= 0

        @pl.when(full)
        def _():
            @pl.when((g > 0) & (g < n - 1))
            def _():
                product((2 * g - 1) * wide, 4 * wide, 0)

            @pl.when(g == 0)
            def _():
                product(0, 3 * wide, wide)
                clear(0)

            @pl.when(g == n - 1)
            def _():
                product((total - 3) * wide, 3 * wide, 0)
                clear(3 * wide)

            product((total + g) * wide, wide, 4 * wide)

        if staged:

            @pl.when(jnp.logical_not(full))
            def _():
                @pl.when(jnp.logical_not(mirror) & (g > 0))
                def _():
                    product((2 * g - 1) * wide, 3 * wide, 0)

                @pl.when(jnp.logical_not(mirror) & (g == 0))
                def _():
                    product(0, 2 * wide, wide)
                    clear(0)

                @pl.when(mirror & (g < n - 1))
                def _():
                    product(2 * g * wide, 3 * wide, wide)

                @pl.when(mirror & (g == n - 1))
                def _():
                    product(2 * g * wide, 2 * wide, wide)
                    clear(3 * wide)

        through = ((g > k) & (k > 0)) | ((g < k) & (k < n - 1))
        into = jnp.where(g == k, n + 1, g)
        if staged:
            does = between | (s < AHEAD) | (g != first_group) | (i >= AHEAD), s >= AHEAD
        else:
            does = s >= 0, s >= 0
        for part in range(2):
            pl.when(through & does[part])(lambda: arrival(g, i, part).wait_recv())

        def move(q, carry):
            here = pl.ds(pl.multiple_of((first_chunk + i) * width + q * LANES, LANES), LANES)
            low, high = [], []
            for e in range(3):
                speed, ahead = speeds[e : e + 1, here], directions[e : e + 1, here] == 1
                low.append(jnp.broadcast_to(jnp.where(ahead, speed, 0.0), (BLOCK, LANES)))
                high.append(jnp.broadcast_to(jnp.where(ahead, 0.0, speed), (BLOCK, LANES)))
            whole = sum(low) + sum(high)
            outer_low = jnp.where(y == 1, low[1], 0.0)
            outer_high = jnp.where(y == 0, high[1], 0.0)
            def quarter(t, row):
                at = spot(t, row)

                @pl.when(((at == 0) & does[0]) | ((at > 0) & does[1]))
                def _():
                    for b in range(LANES // BLOCK):
                        shift = b * BLOCK
                        base = (1 + t) * wide + row * LANES + shift
                        value = sums[q, base : base + BLOCK]
                        before = sums[q, base - 1 : base - 1 + BLOCK]
                        after = sums[q, base + 1 : base + 1 + BLOCK]
                        if b == 0:
                            before = jnp.where(near_row == 0, 0.0, before)
                        if shift + BLOCK == LANES:
                            after = jnp.where(near_row == BLOCK - 1, 0.0, after)
                        side = (1 + t) * wide + (1 - row) * LANES + shift
                        along = sums[q, side : side + BLOCK]
                        edge = 4 * wide + t * LANES + shift
                        halo = sums[q, edge : edge + BLOCK]
                        flow = low[0] * before + high[0] * after
                        if row == 0:
                            flow = flow + outer_low * halo + high[1] * along
                        else:
                            flow = flow + low[1] * along + outer_high * halo
                        flow = flow + low[2] * sums[q, base - wide : base - wide + BLOCK]
                        flow = flow + high[2] * sums[q, base + wide : base + wide + BLOCK]
                        free = fluids[2 * g + t, row * LANES + shift : row * LANES + shift + BLOCK]
                        moved = value - free * (whole * value - flow)
                        there = pl.ds(pl.multiple_of(at * LANES + shift, BLOCK), BLOCK)
                        prior = slots[into, i, q, there].astype(jnp.float32)
                        moved = moved + jnp.where(through, prior, 0.0)
                        slots[into, i, q, there] = moved.astype(jnp.bfloat16)

            for t in range(2):
                for row in range(2):
                    quarter(t, row)
            return carry

        lax.fori_loop(0, strips, move, 0)
        for part in range(2):
            pl.when((g != k) & does[part])(lambda: message(g, i, part).start())

        def conclude(f, carry):
            for part in range(2):
                pl.when(k > 0)(lambda: arrival(k, f, part).wait_recv())
                pl.when(k < n - 1)(lambda: arrival(n, f, part).wait_recv())

            def settle(q, carry):
                for t in range(2):
                    for row in range(2):
                        here = pl.ds(pl.multiple_of(spot(t, row) * LANES, LANES), LANES)
                        low = slots[k, f, q, here].astype(jnp.float32)
                        high = slots[n, f, q, here].astype(jnp.float32)
                        value = slots[n + 1, f, q, here].astype(jnp.float32)
                        value = value + jnp.where(k > 0, low, 0.0) + jnp.where(k < n - 1, high, 0.0)
                        exact = lax.dot_general(
                            unit, value.astype(jnp.bfloat16), (((1,), (1,)), ((), ())),
                            preferred_element_type=jnp.float32,
                        )
                        spaced[pl.ds(t * wide + row, LANES, stride=2), :] = exact
                slots[n + 1, f, q] = spaced[pl.ds(0, 2 * wide), :].astype(jnp.bfloat16)
                return carry

            lax.fori_loop(0, strips, settle, 0)
            keep(f).start()
            give(f).start()
            return carry

        behind = s - last - jnp.where(at == 1, KEPT, 0) if staged else s - last
        low_end = jnp.maximum(behind, 0)
        high_end = jnp.where(s == steps - 1, chunks, jnp.maximum(behind + 1, 0))
        lax.fori_loop(low_end, high_end, conclude, 0)

        return carry

    lax.fori_loop(begin, steps, step, 0)

    def finish(i, carry):
        keep(i).wait()
        give(i).wait_send()
        return carry

    lax.fori_loop(0, chunks, finish, 0)

    def returned(i, carry):
        given(i).wait_recv()
        matrix_send(i).wait_send()
        return carry

    lax.fori_loop(0, other_chunks, returned, 0)

    def sent(g, carry):
        @pl.when(g != k)
        def _():
            def one(m, carry):
                message(g, m, 0).wait_send()
                message(g, m, 1).wait_send()
                return carry

            lax.fori_loop(0, chunks, one, 0)

        return carry

    lax.fori_loop(0, n, sent, 0)
    for j in range(1, total):
        flag_send(j).wait_send()
    for q in range(planes):
        core_own(q).wait_send()
        halo_send(x, q).wait_send()
        halo_pass(x * planes + q).wait_send()
        for m in range(1, groups):
            to = other_group(m)
            main_send(to, q).wait_send()
            halo_send(to, q).wait_send()
            core_pass(to * planes + q).wait_send()
            halo_pass(to * planes + q).wait_send()


def on_device(chips, groups, distribution, collision, speeds, directions, cell_flags):
    planes, depth = distribution.shape[:2]
    matrix = collision.T
    extra = -matrix.shape[1] % LANES
    if extra:
        matrix, speeds, directions = (jnp.pad(v, ((0, 0), (0, extra))) for v in (matrix, speeds, directions))
    velocities = matrix.shape[1]
    width, most = stripes(velocities)
    total = chips * CORES
    wide = 2 * LANES
    dist = distribution.reshape(planes, 2 * depth, LANES)
    fluid = jnp.broadcast_to((1 - cell_flags).astype(jnp.float32).reshape(1, wide), (8, wide))
    any_space = pl.BlockSpec(memory_space=pl.ANY)
    vmem = pl.BlockSpec(memory_space=pltpu.VMEM)
    dma = pltpu.SemaphoreType.DMA
    size = (chips, groups, planes, depth, width, most, velocities // width - most)
    flops = 2 * velocities * depth * 5 * wide * chips
    out, _ = pl.pallas_call(
        functools.partial(kernel, size),
        out_shape=(
            jax.ShapeDtypeStruct((velocities // LANES, wide, LANES), jnp.bfloat16),
            jax.ShapeDtypeStruct((most, depth, width), jnp.bfloat16),
        ),
        in_specs=[any_space, any_space, vmem, vmem, vmem],
        out_specs=(any_space, any_space),
        scratch_shapes=[
            pltpu.VMEM((CORES, (total + chips) * wide, depth), jnp.bfloat16),
            pltpu.VMEM((2, CORES, depth, width), jnp.bfloat16),
            pltpu.VMEM((width // LANES, 5 * wide, LANES), jnp.float32),
            pltpu.VMEM((chips + 2, most, width // LANES, 2 * wide, LANES), jnp.bfloat16),
            pltpu.VMEM((total, 8, wide), jnp.float32),
            pltpu.VMEM((total, wide, LANES), jnp.float32),
            pltpu.VMEM((2, 2 * depth, LANES), jnp.bfloat16),
            pltpu.VMEM((2 * depth, LANES), jnp.float32),
            dma((planes,)),
            dma((total,)), dma((total,)),
            dma((groups, planes)), dma((total,)),
            dma((groups, planes)), dma((total,)),
            dma((total,)), dma((total,)),
            dma((most,)), dma((most,)),
            dma((total,)), dma((total,)),
            dma((2, 2)),
            dma((2, chips, most)), dma((2, chips + 1, most)),
            dma((most,)), dma((most,)), dma((CORES * most,)),
        ],
        compiler_params=pltpu.CompilerParams(
            collective_id=0, has_side_effects=True, vmem_limit_bytes=60 << 20
        ),
        cost_estimate=pl.CostEstimate(flops=flops, bytes_accessed=velocities * depth * 2 * chips, transcendentals=0),
    )(dist, matrix, speeds, directions, fluid)
    return out.reshape(1, velocities, 2, LANES)[:, : velocities - extra]


def solution(mesh):
    return jax.shard_map(
        functools.partial(on_device, mesh.shape["vin"] // CORES, mesh.shape["vout"]),
        mesh=mesh,
        in_specs=(
            P("vout", "vin", "cell", None),
            P("vout", "vin"),
            P(None, "vout"),
            P(None, "vout"),
            P("vin", "cell", None),
        ),
        out_specs=P("vin", "vout", "cell", None),
        check_vma=False,
    )
```

```python
import functools

import jax
import jax.numpy as jnp
from jax import lax
from jax.experimental import pallas as pl
from jax.experimental.pallas import tpu as pltpu
from jax.sharding import PartitionSpec as P

MESH = pl.DeviceIdType.MESH
CORES = 2
LANES = 128
BLOCK = 16
KEPT = 3
AHEAD = 8


def stripes(velocities):
    width = 2 * LANES if velocities % (2 * LANES) == 0 else LANES
    return width, pl.cdiv(velocities // width, CORES)


def kernel(
    size, dist, matrix, speeds, directions, fluid, out, lent,
    held, tile, sums, slots, flat, fluids, raw, spaced,
    l_sem, cs_sem, cr_sem, xs_sem, xr_sem, hs_sem, hr_sem, gs_sem, gr_sem, ms_sem, mr_sem,
    fs_sem, fr_sem, t_sem, zs_sem, zr_sem, ol_sem, os_sem, or_sem,
):
    n, groups, planes, depth, width, most, least = size
    total = n * CORES
    strips = width // LANES
    wide = 2 * LANES
    vin, x, y = lax.axis_index("vin"), lax.axis_index("vout"), lax.axis_index("cell")
    k, c = vin // CORES, lax.rem(vin, CORES)
    partner = {"vin": k * CORES + 1 - c}
    chunks = jnp.where(c == 0, most, least)
    first_chunk, other_first = c * most, (1 - c) * most
    other_chunks = jnp.where(c == 0, least, most)
    mirror = 2 * x >= groups
    staged = groups == 2 and n == 4 and planes == 4

    def remote(src, dst, send, recv, where):
        return pltpu.make_async_remote_copy(
            src_ref=src, dst_ref=dst, send_sem=send, recv_sem=recv, device_id=where, device_id_type=MESH
        )

    def other_group(j):
        return lax.rem(x + j, groups)

    everyone = [{"vin": lax.rem(vin + j, total)} for j in range(1, total)]
    for j in range(groups):
        if j:
            everyone.append({"vout": other_group(j)})
        everyone.append({"vout": other_group(j), "cell": 1 - y})
    barrier = pltpu.get_barrier_semaphore()
    for where in everyone:
        pl.semaphore_signal(barrier, inc=1, device_id=where, device_id_type=MESH)

    at = jnp.where(mirror, n - 1 - k, k)
    final_chip = at == n - 1

    def turned(g):
        return jnp.where(mirror, n - 1 - g, g)

    first_group = turned(jnp.where(at <= 1, 1, 0)) if staged else 0
    steps = n * chunks + AHEAD if staged else n * chunks
    last = steps - chunks

    held_back = jnp.where(at == 0, KEPT, 0)
    share = jnp.where(at == 0, 10, jnp.where(at == 1, 10, 12))
    between = at == 1 if staged else False
    begin = jnp.where(between, AHEAD, 0)

    def item(s):
        if not staged:
            return s // chunks, lax.rem(s, chunks)
        j = s - AHEAD - chunks + held_back
        done = jnp.minimum(share * j // 30, chunks)
        alone = jnp.minimum(share * (j + 1) // 30, chunks) > done
        sent = j - done
        one, over = sent < chunks, sent >= 2 * chunks
        g = jnp.where(one, jnp.where(at == 2, 1, 2), jnp.where(over, 1, 3))
        i = jnp.where(one, sent, jnp.where(over, sent - chunks - KEPT, sent - chunks))
        g = jnp.where(alone, jnp.where(at == 1, 0, at), g)
        i = jnp.where(alone, done, i)
        g = jnp.where(final_chip, 1 + j // chunks, g)
        i = jnp.where(final_chip, lax.rem(j, chunks), i)
        early = j < 0
        return jnp.where(early, first_group, turned(g)), jnp.where(early, jnp.where(s < AHEAD, s, s - AHEAD), i)

    inner, outer = 1 - y, y

    def inner_of(p):
        return pl.ds(pl.multiple_of(p * wide + inner * LANES, LANES), LANES)

    diagonal = lax.broadcasted_iota(jnp.int32, (LANES, LANES), 0) == lax.broadcasted_iota(jnp.int32, (LANES, LANES), 1)
    unit = jnp.where(diagonal, 1.0, 0.0).astype(jnp.bfloat16)

    def flipped(values):
        exact = lax.dot_general(unit, values, (((1,), (1,)), ((), ())), preferred_element_type=jnp.float32)
        return exact.astype(jnp.bfloat16)

    def main_of(p):
        return pl.ds(pl.multiple_of(p * wide, wide), wide)

    def halo_of(p):
        return pl.ds(pl.multiple_of(total * wide + p * LANES, LANES), LANES)

    first_pair = lax.rem(first_group, planes // 2)

    def halo_order(j):
        if not staged:
            return j
        pair = first_pair if j < 2 else 1 - first_pair
        return pair * 2 + j % 2

    def fetch(j):
        return pltpu.make_async_copy(dist.at[halo_order(j)], raw.at[j % 2], l_sem.at[j])

    def turn(j):
        q = halo_order(j)
        spaced[...] = raw[j % 2].astype(jnp.float32)
        for row in range(2):
            values = spaced[pl.ds(row, depth, stride=2), :].astype(jnp.bfloat16)
            at = pl.ds(pl.multiple_of((x * planes + q) * wide + row * LANES, LANES), LANES)
            held[c, at] = flipped(values)

    def core_own(q):
        return core_pass(x * planes + q)

    def core_pass(p):
        return remote(held.at[c, main_of(p)], held.at[c, main_of(p)], cs_sem.at[p], cr_sem.at[p], partner)

    def core_got(p):
        return remote(held.at[1 - c, main_of(p)], held.at[1 - c, main_of(p)], cs_sem.at[p], cr_sem.at[p], partner)

    def main_send(to, q):
        p = x * planes + q
        return remote(held.at[c, main_of(p)], held.at[c, main_of(p)], xs_sem.at[to, q], xr_sem.at[p], {"vout": to})

    def main_got(p):
        return remote(held.at[c, main_of(p)], held.at[c, main_of(p)], xs_sem.at[0, 0], xr_sem.at[p], {"vout": other_group(1)})

    def halo_send(to, q):
        p = x * planes + q
        return remote(
            held.at[c, inner_of(p)], held.at[c, halo_of(p)], hs_sem.at[to, q], hr_sem.at[p],
            {"vout": to, "cell": 1 - y},
        )

    def relay(p):
        to, q = p // planes, planes - 1 - lax.rem(p, planes)
        return remote(
            held.at[c, inner_of(p)], held.at[c, halo_of(p)], hs_sem.at[to, q], hr_sem.at[p], {"cell": 1 - y}
        )

    def halo_got(p):
        ref = held.at[c, halo_of(p)]
        return remote(ref, ref, hs_sem.at[0, 0], hr_sem.at[p], {"cell": 1 - y})

    def halo_pass(p):
        ref = held.at[c, halo_of(p)]
        return remote(ref, ref, gs_sem.at[p], gr_sem.at[p], partner)

    def halo_end(p):
        ref = held.at[1 - c, halo_of(p)]
        return remote(ref, ref, gs_sem.at[p], gr_sem.at[p], partner)

    def lanes_of(chunk):
        return pl.ds(pl.multiple_of(chunk * width, LANES), width)

    def matrix_send(i):
        return remote(
            matrix.at[:, lanes_of(other_first + i)], lent.at[i], ms_sem.at[i], mr_sem.at[i], partner
        )

    def matrix_got(i):
        return remote(lent.at[i], lent.at[i], ms_sem.at[i], mr_sem.at[i], partner)

    def flag_send(j):
        to = lax.rem(vin + j, total)
        return remote(fluid, flat.at[vin], fs_sem.at[to], fr_sem.at[vin], {"vin": to})

    def flag_got(j):
        at = lax.rem(vin + j, total)
        return remote(fluid, flat.at[at], fs_sem.at[at], fr_sem.at[at], {"vin": at})

    def load(s, which):
        i = item(s)[1]
        slot = lax.rem(s, 2)
        if which == 0:
            src, at = matrix.at[:, lanes_of(first_chunk + i)], c
        else:
            src, at = lent.at[i], 1 - c
        return pltpu.make_async_copy(src, tile.at[slot, at], t_sem.at[slot, which])

    def away(to, j):
        return jnp.where(x > to, j, planes - 1 - j)

    def from_group(src, j):
        return src * planes + jnp.where(src > x, j, planes - 1 - j)

    load(begin, 0).start()
    for j in range(min(2, planes)):
        fetch(j).start()
    for j in range(planes):
        fetch(j).wait()
        turn(j)
        if j + 2 < planes:
            fetch(j + 2).start()
        if j == 0:
            pl.semaphore_wait(barrier, len(everyone))
            matrix_send(0).start()
        core_own(halo_order(j)).start()
        if j < 2:
            halo_send(x, halo_order(j)).start()
    for m in range(1, groups):
        to = other_group(m)
        main_send(to, away(to, 0)).start()
    for j in range(1, total):
        flag_send(j).start()

    def lend(i, carry):
        matrix_send(i).start()
        return carry

    lax.fori_loop(1, other_chunks, lend, 0)
    for j in range(2, planes):
        halo_send(x, halo_order(j)).start()
    for m in range(1, groups):
        to = other_group(m)
        for j in range(1, min(3, planes)):
            main_send(to, away(to, j)).start()
        if not staged:
            for j in range(min(2, planes)):
                halo_send(to, away(to, j)).start()
        for j in range(3, planes):
            main_send(to, away(to, j)).start()
        for j in range(2, planes):
            halo_send(to, away(to, j)).start()
    flat[vin] = fluid[...]
    for q in range(strips):
        sums[q, 4 * wide : 5 * wide] = jnp.zeros((wide, LANES), jnp.float32)
    matrix_got(0).wait_recv()
    load(begin, 1).start()
    for j in range(1, total):
        flag_got(j).wait_recv()

    def spread(p, carry):
        for row in range(2):
            line = flat[p, 0:1, row * LANES : (row + 1) * LANES]
            fluids[p, row * LANES : (row + 1) * LANES] = jnp.broadcast_to(line, (LANES, LANES)).T
        return carry

    lax.fori_loop(0, total, spread, 0)

    own = [x * planes + halo_order(j) for j in range(planes)]

    def pass_halo(ps):
        for p in ps:
            halo_got(p).wait_recv()
            halo_pass(p).start()

    def end_halo(ps):
        for p in ps:
            halo_end(p).wait_recv()

    def pass_main(ps):
        for p in ps:
            main_got(p).wait_recv()
            core_pass(p).start()

    def relay_rows(ps):
        for p in ps:
            relay(p).start()

    def end_main(ps):
        for p in ps:
            core_got(p).wait_recv()

    def others(low, high):
        return [from_group(other_group(m), j) for m in range(1, groups) for j in range(low, min(high, planes))]

    near, middle, far, near_halo, far_halo = others(0, 1), others(1, 3), others(3, 99), others(0, 2), others(2, 99)
    end_main([x * planes + q for q in range(planes)])

    def at_step(s):
        def when(step, *calls):
            @pl.when(s == step)
            def _():
                for call, ps in calls:
                    call(ps)

        when(jnp.where(between, AHEAD, AHEAD - 2), (pass_halo, own[:2]), (pass_main, near), (relay_rows, near))
        when(AHEAD, (end_halo, own[:2]), (end_main, near))
        when(AHEAD + 7, (pass_main, middle[:1]), (relay_rows, middle[:1]))
        when(AHEAD + chunks - KEPT - 2, (pass_halo, own[2:]), (pass_main, middle[1:]), (pass_halo, near_halo))
        when(AHEAD + chunks - KEPT, (end_halo, own[2:]))
        when(
            jnp.where(final_chip, AHEAD + 2 * chunks, AHEAD + chunks - KEPT), (end_main, middle), (end_halo, near_halo)
        )
        when(AHEAD + chunks + 12, (pass_main, far), (pass_halo, far_halo))
        when(AHEAD + chunks + 15, (end_main, far), (end_halo, far_halo))

    if not staged:
        pass_halo(own)
        pass_main(near + middle + far)
        pass_halo(near_halo + far_halo)
        end_halo(own)
        end_main(near + middle + far)
        end_halo(near_halo + far_halo)

    near_row = lax.broadcasted_iota(jnp.int32, (BLOCK, LANES), 0)

    parts = (pl.ds(0, LANES), pl.ds(LANES, 3 * LANES))

    def message(g, i, part):
        up = g > k
        chip = jnp.clip(jnp.where(up, k + 1, k - 1), 0, n - 1)
        slot = jnp.where(up | (chip != g), g, n)
        rows = parts[part]
        return remote(
            slots.at[g, i, :, rows], slots.at[slot, i, :, rows], zs_sem.at[part, g, i], zr_sem.at[part, slot, i],
            {"vin": chip * CORES + c},
        )

    def arrival(slot, i, part):
        ref = slots.at[slot, i, :, parts[part]]
        return remote(ref, ref, zs_sem.at[0, 0, 0], zr_sem.at[part, slot, i], partner)

    first_plane = jnp.where(mirror, 1, 0)

    def spot(t, row):
        return jnp.where(first_plane == t, 0, 2) + jnp.where(outer == row, 0, 1)

    def place(chunk):
        return pl.ds(chunk * strips, strips)

    def plane_of(i, at):
        return slots.at[n + 1, i, :, pl.ds(pl.multiple_of(at * wide, wide), wide)]

    def give(i):
        return remote(
            plane_of(i, 1 - c), out.at[place(first_chunk + i)], os_sem.at[i], or_sem.at[first_chunk + i], partner
        )

    def given(i):
        dst = out.at[place(other_first + i)]
        return remote(dst, dst, os_sem.at[i], or_sem.at[other_first + i], partner)

    def keep(i):
        return pltpu.make_async_copy(plane_of(i, c), out.at[place(first_chunk + i)], ol_sem.at[i])

    def step(s, carry):
        g, i = item(s)
        slot = lax.rem(s, 2)
        if staged:
            at_step(s)
        load(s, 0).wait()
        load(s, 1).wait()

        @pl.when(s + 1 < steps)
        def _():
            if staged:
                later = s + 1 - AHEAD
                first_use = jnp.where(between, 1, AHEAD)
                pl.when(later < 0)(lambda: matrix_got(s + 1).wait_recv())
                pl.when((later >= first_use) & (later < chunks - KEPT))(lambda: matrix_got(later).wait_recv())

                @pl.when(later == chunks - KEPT)
                def _():
                    for e in range(KEPT):
                        matrix_got(chunks - KEPT + e).wait_recv()

            else:
                pl.when(s + 1 < chunks)(lambda: matrix_got(s + 1).wait_recv())

            load(s + 1, 0).start()
            load(s + 1, 1).start()

        def product(start, count, to):
            at = pl.ds(pl.multiple_of(start, wide), count)
            value = jnp.dot(held[0, at], tile[slot, 0], preferred_element_type=jnp.float32)
            value = value + jnp.dot(held[1, at], tile[slot, 1], preferred_element_type=jnp.float32)
            for q in range(strips):
                sums[q, to : to + count] = value[:, q * LANES : (q + 1) * LANES]

        def clear(at):
            for q in range(strips):
                sums[q, at : at + wide] = jnp.zeros((wide, LANES), jnp.float32)

        full = s >= AHEAD if staged else s >= 0

        @pl.when(full)
        def _():
            @pl.when((g > 0) & (g < n - 1))
            def _():
                product((2 * g - 1) * wide, 4 * wide, 0)

            @pl.when(g == 0)
            def _():
                product(0, 3 * wide, wide)
                clear(0)

            @pl.when(g == n - 1)
            def _():
                product((total - 3) * wide, 3 * wide, 0)
                clear(3 * wide)

            product((total + g) * wide, wide, 4 * wide)

        if staged:

            @pl.when(jnp.logical_not(full))
            def _():
                @pl.when(jnp.logical_not(mirror) & (g > 0))
                def _():
                    product((2 * g - 1) * wide, 3 * wide, 0)

                @pl.when(jnp.logical_not(mirror) & (g == 0))
                def _():
                    product(0, 2 * wide, wide)
                    clear(0)

                @pl.when(mirror & (g < n - 1))
                def _():
                    product(2 * g * wide, 3 * wide, wide)

                @pl.when(mirror & (g == n - 1))
                def _():
                    product(2 * g * wide, 2 * wide, wide)
                    clear(3 * wide)

        through = ((g > k) & (k > 0)) | ((g < k) & (k < n - 1))
        into = jnp.where(g == k, n + 1, g)
        if staged:
            does = between | (s < AHEAD) | (g != first_group) | (i >= AHEAD), s >= AHEAD
        else:
            does = s >= 0, s >= 0
        for part in range(2):
            pl.when(through & does[part])(lambda: arrival(g, i, part).wait_recv())

        def move(q, carry):
            here = pl.ds(pl.multiple_of((first_chunk + i) * width + q * LANES, LANES), LANES)
            low, high = [], []
            for e in range(3):
                speed, ahead = speeds[e : e + 1, here], directions[e : e + 1, here] == 1
                low.append(jnp.broadcast_to(jnp.where(ahead, speed, 0.0), (BLOCK, LANES)))
                high.append(jnp.broadcast_to(jnp.where(ahead, 0.0, speed), (BLOCK, LANES)))
            whole = sum(low) + sum(high)
            outer_low = jnp.where(y == 1, low[1], 0.0)
            outer_high = jnp.where(y == 0, high[1], 0.0)
            def quarter(t, row):
                at = spot(t, row)

                @pl.when(((at == 0) & does[0]) | ((at > 0) & does[1]))
                def _():
                    for b in range(LANES // BLOCK):
                        shift = b * BLOCK
                        base = (1 + t) * wide + row * LANES + shift
                        value = sums[q, base : base + BLOCK]
                        before = sums[q, base - 1 : base - 1 + BLOCK]
                        after = sums[q, base + 1 : base + 1 + BLOCK]
                        if b == 0:
                            before = jnp.where(near_row == 0, 0.0, before)
                        if shift + BLOCK == LANES:
                            after = jnp.where(near_row == BLOCK - 1, 0.0, after)
                        side = (1 + t) * wide + (1 - row) * LANES + shift
                        along = sums[q, side : side + BLOCK]
                        edge = 4 * wide + t * LANES + shift
                        halo = sums[q, edge : edge + BLOCK]
                        flow = low[0] * before + high[0] * after
                        if row == 0:
                            flow = flow + outer_low * halo + high[1] * along
                        else:
                            flow = flow + low[1] * along + outer_high * halo
                        flow = flow + low[2] * sums[q, base - wide : base - wide + BLOCK]
                        flow = flow + high[2] * sums[q, base + wide : base + wide + BLOCK]
                        free = fluids[2 * g + t, row * LANES + shift : row * LANES + shift + BLOCK]
                        moved = value - free * (whole * value - flow)
                        there = pl.ds(pl.multiple_of(at * LANES + shift, BLOCK), BLOCK)
                        prior = slots[into, i, q, there].astype(jnp.float32)
                        moved = moved + jnp.where(through, prior, 0.0)
                        slots[into, i, q, there] = moved.astype(jnp.bfloat16)

            for t in range(2):
                for row in range(2):
                    quarter(t, row)
            return carry

        lax.fori_loop(0, strips, move, 0)
        for part in range(2):
            pl.when((g != k) & does[part])(lambda: message(g, i, part).start())

        def conclude(f, carry):
            for part in range(2):
                pl.when(k > 0)(lambda: arrival(k, f, part).wait_recv())
                pl.when(k < n - 1)(lambda: arrival(n, f, part).wait_recv())

            def settle(q, carry):
                for t in range(2):
                    for row in range(2):
                        here = pl.ds(pl.multiple_of(spot(t, row) * LANES, LANES), LANES)
                        low = slots[k, f, q, here].astype(jnp.float32)
                        high = slots[n, f, q, here].astype(jnp.float32)
                        value = slots[n + 1, f, q, here].astype(jnp.float32)
                        value = value + jnp.where(k > 0, low, 0.0) + jnp.where(k < n - 1, high, 0.0)
                        exact = lax.dot_general(
                            unit, value.astype(jnp.bfloat16), (((1,), (1,)), ((), ())),
                            preferred_element_type=jnp.float32,
                        )
                        spaced[pl.ds(t * wide + row, LANES, stride=2), :] = exact
                slots[n + 1, f, q] = spaced[pl.ds(0, 2 * wide), :].astype(jnp.bfloat16)
                return carry

            lax.fori_loop(0, strips, settle, 0)
            keep(f).start()
            give(f).start()
            return carry

        behind = s - last - jnp.where((at == 1) | (at == 2), KEPT, 0) if staged else s - last
        low_end = jnp.maximum(behind, 0)
        high_end = jnp.where(s == steps - 1, chunks, jnp.maximum(behind + 1, 0))
        lax.fori_loop(low_end, high_end, conclude, 0)

        return carry

    lax.fori_loop(begin, steps, step, 0)

    def finish(i, carry):
        keep(i).wait()
        give(i).wait_send()
        return carry

    lax.fori_loop(0, chunks, finish, 0)

    def returned(i, carry):
        given(i).wait_recv()
        matrix_send(i).wait_send()
        return carry

    lax.fori_loop(0, other_chunks, returned, 0)

    def sent(g, carry):
        @pl.when(g != k)
        def _():
            def one(m, carry):
                message(g, m, 0).wait_send()
                message(g, m, 1).wait_send()
                return carry

            lax.fori_loop(0, chunks, one, 0)

        return carry

    lax.fori_loop(0, n, sent, 0)
    for j in range(1, total):
        flag_send(j).wait_send()
    for q in range(planes):
        core_own(q).wait_send()
        halo_send(x, q).wait_send()
        halo_pass(x * planes + q).wait_send()
        for m in range(1, groups):
            to = other_group(m)
            main_send(to, q).wait_send()
            halo_send(to, q).wait_send()
            core_pass(to * planes + q).wait_send()
            halo_pass(to * planes + q).wait_send()


def on_device(chips, groups, distribution, collision, speeds, directions, cell_flags):
    planes, depth = distribution.shape[:2]
    matrix = collision.T
    extra = -matrix.shape[1] % LANES
    if extra:
        matrix, speeds, directions = (jnp.pad(v, ((0, 0), (0, extra))) for v in (matrix, speeds, directions))
    velocities = matrix.shape[1]
    width, most = stripes(velocities)
    total = chips * CORES
    wide = 2 * LANES
    dist = distribution.reshape(planes, 2 * depth, LANES)
    fluid = jnp.broadcast_to((1 - cell_flags).astype(jnp.float32).reshape(1, wide), (8, wide))
    any_space = pl.BlockSpec(memory_space=pl.ANY)
    vmem = pl.BlockSpec(memory_space=pltpu.VMEM)
    dma = pltpu.SemaphoreType.DMA
    size = (chips, groups, planes, depth, width, most, velocities // width - most)
    flops = 2 * velocities * depth * 5 * wide * chips
    out, _ = pl.pallas_call(
        functools.partial(kernel, size),
        out_shape=(
            jax.ShapeDtypeStruct((velocities // LANES, wide, LANES), jnp.bfloat16),
            jax.ShapeDtypeStruct((most, depth, width), jnp.bfloat16),
        ),
        in_specs=[any_space, any_space, vmem, vmem, vmem],
        out_specs=(any_space, any_space),
        scratch_shapes=[
            pltpu.VMEM((CORES, (total + chips) * wide, depth), jnp.bfloat16),
            pltpu.VMEM((2, CORES, depth, width), jnp.bfloat16),
            pltpu.VMEM((width // LANES, 5 * wide, LANES), jnp.float32),
            pltpu.VMEM((chips + 2, most, width // LANES, 2 * wide, LANES), jnp.bfloat16),
            pltpu.VMEM((total, 8, wide), jnp.float32),
            pltpu.VMEM((total, wide, LANES), jnp.float32),
            pltpu.VMEM((2, 2 * depth, LANES), jnp.bfloat16),
            pltpu.VMEM((2 * depth, LANES), jnp.float32),
            dma((planes,)),
            dma((total,)), dma((total,)),
            dma((groups, planes)), dma((total,)),
            dma((groups, planes)), dma((total,)),
            dma((total,)), dma((total,)),
            dma((most,)), dma((most,)),
            dma((total,)), dma((total,)),
            dma((2, 2)),
            dma((2, chips, most)), dma((2, chips + 1, most)),
            dma((most,)), dma((most,)), dma((CORES * most,)),
        ],
        compiler_params=pltpu.CompilerParams(
            collective_id=0, has_side_effects=True, vmem_limit_bytes=60 << 20
        ),
        cost_estimate=pl.CostEstimate(flops=flops, bytes_accessed=velocities * depth * 2 * chips, transcendentals=0),
    )(dist, matrix, speeds, directions, fluid)
    return out.reshape(1, velocities, 2, LANES)[:, : velocities - extra]


def solution(mesh):
    return jax.shard_map(
        functools.partial(on_device, mesh.shape["vin"] // CORES, mesh.shape["vout"]),
        mesh=mesh,
        in_specs=(
            P("vout", "vin", "cell", None),
            P("vout", "vin"),
            P(None, "vout"),
            P(None, "vout"),
            P("vin", "cell", None),
        ),
        out_specs=P("vin", "vout", "cell", None),
        check_vma=False,
    )
```
